32 devices in a mesh: groups: 2 (over y), dev: 4 (over z), pd: 4 (over x, core).
Axes of the slice: x: 2, y: 2, z: 4, core: 2. Of those that a mesh axis runs over, the one named last changes fastest.
Arguments:
- queries: bfloat16 [64, 4, 16, 192], P(('groups', 'dev', 'pd')), parts along dimension 0, may hold values from -250 to 250
- new_latents: bfloat16 [64, 4, 576], P(('groups', 'dev', 'pd')), parts along dimension 0, may hold values from -4 to 4
- prompt_blocks: bfloat16 [512, 128, 576], P(('groups', 'dev', 'pd')), parts along dimension 0, may hold values from -6 to 6
- block_routes: int32 [512, 3], P(('groups', 'dev', 'pd')), parts along dimension 0, may hold values from 0 to 31, as said below
- prompt_lengths: int32 [64], P(('groups', 'dev', 'pd')), parts along dimension 0, may hold values from 0 to 4096, as said below
- resident_blocks: bfloat16 [512, 128, 576], P(('groups', 'dev', 'pd')), parts along dimension 0, may hold values from -6 to 6
- resident_slots: int32 [512], P(('groups', 'dev', 'pd')), parts along dimension 0, may hold values from 0 to 1
- key_absorb: bfloat16 [16, 128, 512], P('dev'), may hold values from -0.5 to 0.5
- value_expand: bfloat16 [16, 512, 128], P('dev'), may hold values from -6 to 6
- output_weight: bfloat16 [2048, 7168], P('dev'), may hold values from -0.125 to 0.125
Outputs:
- mixed: bfloat16 [256, 7168], P(('groups', 'dev', 'pd')), parts along dimension 0
The draws below stay inside these ranges and needn't reach their ends.
There are 2 independent parts, one for each index of `groups`. The reference program is written for one: setup_inputs(seed, part) draws one part's arguments, and reference() takes and returns one part's arrays. A program takes and returns all parts, laid end to end along the dimension named above; an argument that names none is the same for every part. Nothing has to cross between parts.
Inputs may be any that keep to these rules, and one draw needn't show every extreme that they name: block_routes[b] = (destination dev index in the holder's pd row, request slot below 2, position of the block in its request's prompt). At most 8 blocks of one device go to one destination, and in every pd row some device receives exactly 8 blocks from every device. The positions of one request's blocks are 0, 1, 2, ... without gaps, in order of holder. `prompt_lengths`: a request with k prompt blocks has a length of 128 * (k - 1) + 1 to 128 * k, and 0 when k = 0.
All inputs are finite; a program needn't handle non-finite values.
Results may differ from the reference program's by a relative error of at most 0.017.
Values may be sent and summed in bfloat16 or wider, within the bound.
A program may use at most 128 MiB of HBM per device.

```python
import math
import jax
import jax.numpy as jnp
from jax import lax

D = 7168
KVR = 512
ROPE = 64
NOPE = 128
VHEAD = 128
H = 16
LAT = 576
QHD = 192
BLOCK = 128
STEPS = 4
REQ_DEV = 2
PBLK_DEV = 16
RES_BLK = 16
CAP = 8
SLOTS = 32
REQS = 32
ROWS = 128
PBLKS = 256
RBLKS = 256
N_DEV = 4
N_PD = 4


def route_plan(key):
    key = jax.random.fold_in(key, 101)

    def one_row(row_key):
        keys = jax.random.split(row_key, 5)
        target = jax.random.randint(keys[0], (), 0, N_DEV)
        places = jnp.arange(SLOTS, dtype=jnp.int32)
        forced = places[None, :] // CAP == target
        scores = jax.random.randint(keys[1], (N_DEV, SLOTS), 0, 2 ** 20) * SLOTS + places[None, :]
        scores = jnp.where(forced, places[None, :] - SLOTS, scores)
        chosen = jnp.argsort(scores, axis=1)[:, :PBLK_DEV]
        shuffle = jax.random.randint(keys[2], (N_DEV, PBLK_DEV), 0, 2 ** 20) * PBLK_DEV + jnp.arange(PBLK_DEV)[None, :]
        chosen = jnp.take_along_axis(chosen, jnp.argsort(shuffle, axis=1), axis=1)
        destination = (chosen // CAP).astype(jnp.int32)
        slots = jax.random.randint(keys[3], (N_DEV, PBLK_DEV), 0, REQ_DEV)
        slots = jnp.where(destination == target, 0, slots).astype(jnp.int32)
        labels = (destination * REQ_DEV + slots).reshape(-1)
        onehot = (labels[:, None] == jnp.arange(N_DEV * REQ_DEV)[None, :]).astype(jnp.int32)
        before = jnp.cumsum(onehot, axis=0) - onehot
        position = jnp.sum(before * onehot, axis=1).reshape(N_DEV, PBLK_DEV)
        counts = jnp.sum(onehot, axis=0).reshape(N_DEV, REQ_DEV)
        extra = jax.random.randint(keys[4], (N_DEV, REQ_DEV), 1, BLOCK + 1)
        lengths = jnp.where(counts > 0, (counts - 1) * BLOCK + extra, 0)
        filled = (jnp.arange(N_DEV)[:, None] == target) & (jnp.arange(REQ_DEV)[None, :] == 0)
        lengths = jnp.where(filled, counts * BLOCK, lengths)
        routes = jnp.stack([destination, slots, position.astype(jnp.int32)], axis=-1)
        return (routes, lengths.astype(jnp.int32))
    routes, lengths = jax.vmap(one_row)(jax.random.split(key, N_PD))
    routes = jnp.transpose(routes, (1, 0, 2, 3)).reshape(N_DEV * N_PD * PBLK_DEV, 3)
    lengths = jnp.transpose(lengths, (1, 0, 2)).reshape(-1)
    return (routes.astype(jnp.int32), lengths.astype(jnp.int32))


def latent_base(key):
    key = jax.random.fold_in(key, 7)
    return jnp.clip(jax.random.normal(key, (REQS, STEPS, LAT), jnp.float32), -4.0, 4.0)


def draw_block_routes(key, part):
    shared = route_plan(key)
    return shared[0]


def draw_prompt_lengths(key, part):
    shared = route_plan(key)
    return shared[1]


def draw_new_latents(key, part):
    base = latent_base(key)
    return base.astype(jnp.bfloat16)


def draw_queries(key, part):
    key = jax.random.fold_in(key, 17)
    keys = jax.random.split(key, 1)
    values = jnp.clip(jax.random.normal(keys[0], (REQS, STEPS, H, QHD), jnp.float32), -5.0, 5.0)
    return values.astype(jnp.bfloat16)


def with_ends(array, stream_key, least, largest):
    dims = array.shape
    spot = [jax.random.randint(jax.random.fold_in(stream_key, axis), (), 0, dims[axis]) for axis in range(len(dims))]
    array = array.at[tuple(spot)].set(least)
    longest = dims.index(max(dims))
    spot[longest] = (spot[longest] + 1) % dims[longest]
    return array.at[tuple(spot)].set(largest)


def block_levels(key, shape, cuts, smallest, high):
    def one(axis_at, blocks):
        heights = jax.random.uniform(jax.random.fold_in(jax.random.fold_in(key, 6), axis_at), (blocks,), jnp.float32, smallest / len(cuts), high / len(cuts))
        return jnp.repeat(jnp.exp(heights), shape[axis_at] // blocks).reshape((-1,) + (1,) * (len(shape) - axis_at - 1))

    factor_of = one(*cuts[0])
    for cut in cuts[1:]:
        factor_of = factor_of * one(*cut)
    return factor_of


def centred(stream_key, extent, deviation, reach, cuts=(), held_as=jnp.bfloat16):
    array = jax.random.normal(stream_key, extent, jnp.float32) * deviation
    if len(cuts) > 0:
        array = block_levels(stream_key, extent, cuts, -0.22, 0.18) * array
    return jnp.clip(array, min=-reach, max=reach).astype(held_as)


def setup_inputs(seed: int = 0, part: int = 0) -> dict:
    splits = jax.random.split(jax.random.key(seed), 11)
    part_splits = jax.random.split(jax.random.fold_in(splits[10], part), 11)
    return {
        "queries": draw_queries(jax.random.fold_in(jax.random.fold_in(splits[10], part), 71), part),
        "new_latents": draw_new_latents(jax.random.fold_in(jax.random.fold_in(splits[10], part), 71), part),
        "prompt_blocks": centred(part_splits[2], (PBLKS, BLOCK, LAT), 1.0, 6.0, ((0, 16),)),
        "block_routes": draw_block_routes(jax.random.fold_in(jax.random.fold_in(splits[10], part), 71), part),
        "prompt_lengths": draw_prompt_lengths(jax.random.fold_in(jax.random.fold_in(splits[10], part), 71), part),
        "resident_blocks": centred(part_splits[5], (RBLKS, BLOCK, LAT), 1.0, 6.0, ((0, 16),)),
        "resident_slots": with_ends(jax.random.randint(part_splits[6], (RBLKS,), 0, REQ_DEV), jax.random.fold_in(part_splits[6], 1), 0, REQ_DEV - 1).astype(jnp.int32),
        "key_absorb": centred(splits[7], (H, NOPE, KVR), NOPE ** -0.5, 0.5, ((0, 4),)),
        "value_expand": centred(splits[8], (H, KVR, VHEAD), 1.0, 6.0, ((0, 4),)),
        "output_weight": centred(splits[9], (H * VHEAD, D), (H * VHEAD) ** -0.5, 0.125, ((0, 4),)),
    }


def absorb_rows(query_rows, key_absorb):
    latent = jnp.einsum('rshn,hnc->rshc', query_rows[..., :NOPE].astype(jnp.float32), key_absorb.astype(jnp.float32))
    return jnp.concatenate([latent.astype(jnp.bfloat16), query_rows[..., NOPE:]], axis=-1)

def attend(absorbed, fresh, blocks, owners, valid):
    scale = 1.0 / math.sqrt(NOPE + ROPE)
    width = STEPS * H
    flat = absorbed.reshape(REQ_DEV, width, LAT)
    opening = jnp.einsum('rqc,rkc->rqk', flat.astype(jnp.float32), fresh.astype(jnp.float32)) * scale
    causal = jnp.arange(STEPS)[None, :] <= (jnp.arange(width) // H)[:, None]
    opening = jnp.where(causal[None], opening, -1e+30)
    picked = jnp.take(flat, owners, axis=0)
    scores = jnp.einsum('gqc,gkc->gqk', picked.astype(jnp.float32), blocks.astype(jnp.float32)) * scale
    live = jnp.arange(BLOCK)[None, :] < valid[:, None]
    scores = jnp.where(live[:, None, :], scores, -1e+30)
    owned = owners[:, None] == jnp.arange(REQ_DEV)[None, :]
    block_top = lax.optimization_barrier(jnp.max(jnp.where(owned[:, :, None], lax.optimization_barrier(jnp.max(scores, axis=2))[:, None, :], -1e+30), axis=0))
    top = jnp.maximum(lax.optimization_barrier(jnp.max(opening, axis=2)), block_top)
    first = jnp.where(causal[None], jnp.exp(opening - top[..., None]), 0.0)
    weight = jnp.where(live[:, None, :], jnp.exp(scores - jnp.take(top, owners, axis=0)[:, :, None]), 0.0)
    ownf = owned.astype(jnp.float32)
    denominator = lax.optimization_barrier(jnp.sum(first, axis=2)) + jnp.einsum('gr,gq->rq', ownf, lax.optimization_barrier(jnp.sum(weight, axis=2)))
    carried = jnp.einsum('gqk,gkc->gqc', weight.astype(jnp.bfloat16).astype(jnp.float32), blocks[..., :KVR].astype(jnp.float32))
    numerator = jnp.einsum('rqk,rkc->rqc', first.astype(jnp.bfloat16).astype(jnp.float32), fresh[..., :KVR].astype(jnp.float32))
    numerator = numerator + jnp.einsum('gr,gqc->rqc', ownf, carried)
    return (numerator / denominator[..., None]).astype(jnp.bfloat16).reshape(REQ_DEV, STEPS, H, KVR)

def reference(queries, new_latents, prompt_blocks, block_routes, prompt_lengths, resident_blocks, resident_slots, key_absorb, value_expand, output_weight):
    table_all = block_routes.reshape(N_DEV, N_PD, PBLK_DEV, 3)

    def one_device(shard):
        target = shard // N_PD
        row = shard % N_PD
        first_req = shard * REQ_DEV
        query_rows = lax.dynamic_slice_in_dim(queries, first_req, REQ_DEV, 0)
        absorbed = absorb_rows(query_rows, key_absorb)
        fresh = lax.dynamic_slice_in_dim(new_latents, first_req, REQ_DEV, 0)
        lengths = lax.dynamic_slice_in_dim(prompt_lengths, first_req, REQ_DEV, 0)
        home_blocks = lax.dynamic_slice_in_dim(resident_blocks, shard * RES_BLK, RES_BLK, 0)
        home_slots = lax.dynamic_slice_in_dim(resident_slots, shard * RES_BLK, RES_BLK, 0)
        table = jnp.take(table_all, row, axis=1)
        match = (table[..., 0] == target).astype(jnp.int32)
        rank = jnp.cumsum(match, axis=1) - match
        holders = jnp.arange(N_DEV, dtype=jnp.int32)
        gathered = [home_blocks]
        slot_list = [home_slots.astype(jnp.int32)]
        valid_list = [jnp.full((RES_BLK,), BLOCK, jnp.int32)]
        for which in range(CAP):
            hit = match * (rank == which).astype(jnp.int32)
            present = lax.optimization_barrier(jnp.max(hit, axis=1))
            position = jnp.argmax(hit, axis=1).astype(jnp.int32)
            index = ((holders * N_PD + row) * PBLK_DEV + position).astype(jnp.int32)
            gathered.append(jnp.take(prompt_blocks, index, axis=0))
            entry = jnp.take_along_axis(table, position[:, None, None], axis=1)[:, 0]
            slot_now = entry[:, 1].astype(jnp.int32)
            length_now = jnp.take(lengths, slot_now)
            valid_list.append(present * jnp.clip(length_now - BLOCK * entry[:, 2], 0, BLOCK))
            slot_list.append(slot_now)
        blocks = jnp.concatenate(gathered, axis=0)
        owners = jnp.concatenate(slot_list, axis=0)
        valid = jnp.concatenate(valid_list, axis=0).astype(jnp.int32)
        return attend(absorbed, fresh, blocks, owners, valid)
    latent_out = lax.map(one_device, jnp.arange(N_DEV * N_PD, dtype=jnp.int32))
    latent_out = latent_out.reshape(REQS, STEPS, H, KVR)
    expanded = jnp.einsum('rshc,hcv->rshv', latent_out.astype(jnp.float32), value_expand.astype(jnp.float32)).astype(jnp.bfloat16)
    mixed = jnp.dot(expanded.reshape(ROWS, H * VHEAD), output_weight, preferred_element_type=jnp.float32)
    return mixed.astype(jnp.bfloat16)
```

```python
import functools
import math

import jax
import jax.numpy as jnp
from jax import lax
from jax.experimental import pallas as pl
from jax.experimental.pallas import tpu as pltpu
from jax.sharding import PartitionSpec as P

KVR = 512


def deliver(prompt_blocks, block_routes, prompt_lengths):
    devices = lax.axis_size("dev")
    held = prompt_blocks.shape[0]
    width = prompt_blocks.shape[1]
    per_pair = max(1, 2 * held // devices)
    places = devices * per_pair
    destination = block_routes[:, 0]
    mine = (destination[:, None] == jnp.arange(devices, dtype=jnp.int32)[None, :]).astype(jnp.int32)
    rank = jnp.sum((jnp.cumsum(mine, axis=0) - mine) * mine, axis=1)
    position = destination * per_pair + rank
    select = jnp.arange(places, dtype=jnp.int32)[:, None] == position[None, :]
    outgoing = jnp.einsum(
        "sp,pbc->sbc",
        select.astype(jnp.bfloat16),
        prompt_blocks,
        preferred_element_type=jnp.float32,
    ).astype(jnp.bfloat16)
    marks = jnp.concatenate([jnp.ones((held, 1), jnp.int32), block_routes[:, 1:3]], axis=1)
    labels = jnp.sum(select.astype(jnp.int32)[:, :, None] * marks[None, :, :], axis=1)
    arrived, tags = (
        lax.all_to_all(
            outgoing.reshape(devices, per_pair, width, -1),
            "dev",
            split_axis=0,
            concat_axis=0,
            tiled=True,
        ),
        lax.all_to_all(
            labels.reshape(devices, per_pair, 3), "dev", split_axis=0, concat_axis=0, tiled=True
        ),
    )
    arrived = arrived.reshape(places, width, -1)
    tags = tags.reshape(places, 3)
    owners = tags[:, 1]
    requests = prompt_lengths.shape[0]
    lengths = jnp.sum(
        jnp.where(
            owners[:, None] == jnp.arange(requests, dtype=jnp.int32)[None, :],
            prompt_lengths[None, :],
            0,
        ),
        axis=1,
    )
    valid = tags[:, 0] * jnp.clip(lengths - width * tags[:, 2], 0, width)
    return (arrived, owners, valid)


def opening(queries, fresh, heads, scale):
    scores = jnp.einsum("rqc,rkc->rqk", queries, fresh, preferred_element_type=jnp.float32) * scale
    causal = jnp.arange(fresh.shape[1])[None, :] <= (jnp.arange(queries.shape[1]) // heads)[:, None]
    scores = jnp.where(causal[None], scores, -1e30)
    top = jnp.max(scores, axis=2)
    weight = jnp.where(causal[None], jnp.exp(scores - top[..., None]), 0.0)
    total = jnp.sum(weight, axis=2)
    carried = jnp.einsum(
        "rqk,rkc->rqc",
        weight.astype(jnp.bfloat16),
        fresh[..., :KVR],
        preferred_element_type=jnp.float32,
    )
    return (top, total, carried)


def sweep(state, queries, blocks, owners, valid, scale):
    count = blocks.shape[0]
    group = math.gcd(count, 8)
    rounds = count // group
    width = blocks.shape[1]
    requests = queries.shape[0]
    grouped = (
        blocks.reshape(rounds, group, width, blocks.shape[2]),
        owners.reshape(rounds, group),
        valid.reshape(rounds, group),
    )

    def advance(carry, piece):
        top, total, accum = carry
        block_keys, block_owner, block_valid = piece
        picked = jnp.take(queries, block_owner, axis=0)
        scores = (
            jnp.einsum("gqc,gkc->gqk", picked, block_keys, preferred_element_type=jnp.float32)
            * scale
        )
        live = jnp.arange(width)[None, :] < block_valid[:, None]
        scores = jnp.where(live[:, None, :], scores, -1e30)
        owned = block_owner[:, None] == jnp.arange(requests, dtype=jnp.int32)[None, :]
        best = jnp.max(
            jnp.where(owned[:, :, None], jnp.max(scores, axis=2)[:, None, :], -1e30), axis=0
        )
        new_top = jnp.maximum(top, best)
        weight = jnp.where(
            live[:, None, :],
            jnp.exp(scores - jnp.take(new_top, block_owner, axis=0)[:, :, None]),
            0.0,
        )
        ownf = owned.astype(jnp.float32)
        mass = jnp.einsum("gr,gq->rq", ownf, jnp.sum(weight, axis=2))
        carried = jnp.einsum(
            "gqk,gkc->gqc",
            weight.astype(jnp.bfloat16),
            block_keys[..., :KVR],
            preferred_element_type=jnp.float32,
        )
        factor = jnp.exp(top - new_top)
        total = total * factor + mass
        accum = accum * factor[..., None] + jnp.einsum("gr,gqc->rqc", ownf, carried)
        return ((new_top, total, accum), None)

    state, unused = lax.scan(advance, state, grouped)
    return state


def routed_shards(
    queries,
    new_latents,
    prompt_blocks,
    block_routes,
    prompt_lengths,
    resident_blocks,
    resident_slots,
    key_absorb,
    value_expand,
    output_weight,
):
    requests = queries.shape[0]
    steps = queries.shape[1]
    split_at = key_absorb.shape[1]
    scale = 1.0 / math.sqrt(queries.shape[3])
    piece = lax.all_to_all(queries, "dev", split_axis=2, concat_axis=0, tiled=True)
    latent = jnp.einsum(
        "rshn,hnc->rshc", piece[..., :split_at], key_absorb, preferred_element_type=jnp.float32
    ).astype(jnp.bfloat16)
    joined = jnp.concatenate([latent, piece[..., split_at:]], axis=-1)
    absorbed = lax.all_to_all(joined, "dev", split_axis=0, concat_axis=2, tiled=True)
    heads = absorbed.shape[2]
    flat_queries = absorbed.reshape(requests, steps * heads, absorbed.shape[3])
    state = opening(flat_queries, new_latents, heads, scale)
    home_valid = jnp.full((resident_blocks.shape[0],), resident_blocks.shape[1], jnp.int32)
    arrived, owners, valid = deliver(prompt_blocks, block_routes, prompt_lengths)
    joined_blocks = jnp.concatenate([resident_blocks, arrived], axis=0)
    joined_owners = jnp.concatenate([resident_slots, owners], axis=0)
    joined_valid = jnp.concatenate([home_valid, valid], axis=0)
    state = sweep(state, flat_queries, joined_blocks, joined_owners, joined_valid, scale)
    top, total, accum = state
    latent_out = (accum / total[..., None]).astype(jnp.bfloat16).reshape(requests, steps, heads, -1)
    expanded = jnp.einsum(
        "rshc,hcv->rshv",
        lax.all_to_all(latent_out, "dev", split_axis=2, concat_axis=0, tiled=True),
        value_expand,
        preferred_element_type=jnp.float32,
    ).astype(jnp.bfloat16)
    flat = expanded.reshape(expanded.shape[0] * steps, -1)
    mixed = lax.psum_scatter(
        jnp.dot(flat, output_weight, preferred_element_type=jnp.float32).astype(jnp.bfloat16),
        "dev",
        scatter_dimension=0,
        tiled=True,
    )
    return mixed


DEVS = 4
CHUNK = 1024
FAR = -1e30
MESH = pl.DeviceIdType.MESH


def partner(me, step):
    return (me, me + 1 - 2 * (me % 2), (me + 2) % 4, 3 - me)[step]


def still_kernel(
    routes,
    slots,
    lengths,
    queries,
    fresh,
    prompt_hbm,
    resident_hbm,
    absorb_hbm,
    expand_hbm,
    output_hbm,
    out,
    keys,
    absorb,
    expand,
    weight,
    asked,
    lens,
    absorbed,
    bias,
    scores,
    partial,
    stats,
    landed,
    landed_stats,
    mixed,
    landed_mixed,
    local_sem,
    q_send,
    q_recv,
    n_send,
    n_recv,
    a_send,
    a_recv,
    o_send,
    o_recv,
    t_send,
    t_recv,
    y_send,
    y_recv,
    *,
    scale,
):
    me = lax.axis_index("dev")
    prompt_rows = prompt_hbm.shape[0]
    home_rows = resident_hbm.shape[0]
    block = 128
    new_rows = fresh.shape[0]
    heads, nope, rank = absorb.shape
    lat = keys.shape[1]
    own = queries.shape[1] // heads
    rows = DEVS * own
    span = heads * rows
    steps = new_rows // lengths.shape[0]
    requests = lengths.shape[0]

    loads = [
        pltpu.make_async_copy(absorb_hbm, absorb, local_sem.at[0]),
        pltpu.make_async_copy(prompt_hbm, keys.at[pl.ds(0, prompt_rows)], local_sem.at[1]),
        pltpu.make_async_copy(resident_hbm, keys.at[pl.ds(prompt_rows, home_rows)], local_sem.at[2]),
        pltpu.make_async_copy(expand_hbm, expand, local_sem.at[3]),
        pltpu.make_async_copy(output_hbm, weight, local_sem.at[4]),
    ]
    for load in loads:
        load.start()

    barrier = pltpu.get_barrier_semaphore()
    for step in range(1, DEVS):
        pl.semaphore_signal(barrier, inc=1, device_id={"dev": partner(me, step)}, device_id_type=MESH)
    pl.semaphore_wait(barrier, DEVS - 1)

    def remote(source, target, send, recv, step):
        return pltpu.make_async_remote_copy(
            src_ref=source,
            dst_ref=target,
            send_sem=send,
            recv_sem=recv,
            device_id={"dev": partner(me, step)},
            device_id_type=MESH,
        )

    sent = []

    def launch(copy):
        copy.start()
        sent.append(copy)
        return copy

    asks = {}
    for step in (3, 2, 1):
        asks[step] = launch(
            remote(queries.at[partner(me, step)], asked.at[step], q_send.at[step], q_recv.at[step], step)
        )
    request_row = lax.broadcasted_iota(jnp.int32, (own, 128), 0) // steps
    length_rows = jnp.zeros((own, 128), jnp.int32)
    for r in range(requests):
        length_rows = jnp.where(request_row == r, lengths[r], length_rows)
    lens[0] = length_rows
    counts = {}
    for step in (3, 2, 1):
        counts[step] = launch(remote(lens.at[0], lens.at[step], n_send.at[step], n_recv.at[step], step))

    asked[0] = queries[me]
    padding = jnp.zeros((block - new_rows, lat), jnp.float32)
    keys[pl.ds(prompt_rows + home_rows, block), :] = jnp.concatenate(
        [fresh[...].astype(jnp.float32), padding], axis=0
    ).astype(keys.dtype)

    for step in (1, 2, 3):
        asks[step].wait_recv()
    loads[0].wait()
    asking = [asked[step].astype(jnp.float32) for step in range(DEVS)]
    for head in range(heads):
        piece = jnp.concatenate([a[head * own : (head + 1) * own] for a in asking], axis=0).astype(
            jnp.bfloat16
        )
        latent = jnp.dot(piece[:, :nope], absorb[head], preferred_element_type=jnp.float32)
        absorbed[0, pl.ds(head * rows, rows), 0:rank] = latent.astype(jnp.bfloat16)
        absorbed[0, pl.ds(head * rows, rows), rank:lat] = piece[:, nope:]
    shares = {}
    for step in (1, 3, 2):
        shares[step] = launch(
            remote(absorbed.at[0], absorbed.at[step], a_send.at[step], a_recv.at[step], step)
        )

    for step in (1, 2, 3):
        counts[step].wait_recv()
    lane = lax.broadcasted_iota(jnp.int32, (rows, block), 1)
    row = lax.broadcasted_iota(jnp.int32, (rows, block), 0)
    row_length = jnp.concatenate([lens[step] for step in range(DEVS)], axis=0)
    row_device = jnp.zeros((rows, block), jnp.int32)
    for step in range(DEVS):
        row_device = jnp.where(row // own == step, partner(me, step), row_device)
    row_request = row_device * requests + (row % own) // steps
    for b in range(prompt_rows // block):
        owner = routes[3 * b] * requests + routes[3 * b + 1]
        seen = (row_request == owner) & (routes[3 * b + 2] * block + lane < row_length)
        bias[:, pl.ds(b * block, block)] = jnp.where(seen, 0.0, FAR)
    for b in range(home_rows // block):
        seen = row_request == me * requests + slots[b]
        bias[:, pl.ds(prompt_rows + b * block, block)] = jnp.where(seen, 0.0, FAR)
    seen = (
        (row_request == me * requests + lane // steps)
        & (lane % steps <= row % steps)
        & (lane < new_rows)
    )
    total_rows = prompt_rows + home_rows + block
    bias[:, pl.ds(prompt_rows + home_rows, block)] = jnp.where(seen, 0.0, FAR)
    loads[1].wait()
    loads[2].wait()

    cuts = [(at, min(CHUNK, total_rows - at)) for at in range(0, total_rows, CHUNK)]
    for step in (0, 1, 3, 2):
        if step:
            shares[step].wait_recv()
        shard = absorbed[step]
        top = jnp.full((span, 1), FAR, jnp.float32)
        order = [s ^ step for s in range(DEVS)]
        for at, size in cuts:
            piece = lax.dot_general(
                shard,
                keys[pl.ds(at, size), :],
                (((1,), (1,)), ((), ())),
                preferred_element_type=jnp.float32,
            )
            mask = jnp.concatenate(
                [bias[s * own : (s + 1) * own, at : at + size] for s in order], axis=0
            )
            piece = (piece * scale).reshape(heads, rows, size) + mask[None]
            piece = piece.reshape(span, size)
            scores[:, pl.ds(at, size)] = piece
            top = jnp.maximum(top, jnp.max(piece, axis=1, keepdims=True))
        total = jnp.zeros((span, 1), jnp.float32)
        summed = jnp.zeros((span, rank), jnp.float32)
        for at, size in cuts:
            live = jnp.exp(scores[:, pl.ds(at, size)] - top)
            total = total + jnp.sum(live, axis=1, keepdims=True)
            summed = summed + jnp.dot(
                live.astype(jnp.bfloat16),
                keys[pl.ds(at, size), 0:rank],
                preferred_element_type=jnp.float32,
            )
        result = (summed / total).astype(jnp.bfloat16)
        top_row = jnp.transpose(jnp.broadcast_to(top, (span, 128)))[0:8]
        total_row = jnp.transpose(jnp.broadcast_to(total, (span, 128)))[0:8]
        if step:
            partial[step] = result
            stats[step, 0:8, :] = top_row
            stats[step, 8:16, :] = total_row
            launch(remote(stats.at[step], landed_stats.at[step], t_send.at[step], t_recv.at[step], step))
            launch(remote(partial.at[step], landed.at[step], o_send.at[step], o_recv.at[step], step))
        else:
            landed[0] = result
            landed_stats[0, 0:8, :] = top_row
            landed_stats[0, 8:16, :] = total_row

    for step in (1, 3, 2):
        remote(stats.at[step], landed_stats.at[step], t_send.at[step], t_recv.at[step], step).wait_recv()
        remote(partial.at[step], landed.at[step], o_send.at[step], o_recv.at[step], step).wait_recv()
    tops = [
        jnp.transpose(jnp.broadcast_to(landed_stats[s, 0:1, :], (128, span)))[:, 0:1] for s in range(DEVS)
    ]
    totals = [
        jnp.transpose(jnp.broadcast_to(landed_stats[s, 8:9, :], (128, span)))[:, 0:1] for s in range(DEVS)
    ]
    best = functools.reduce(jnp.maximum, tops)
    parts = [t * jnp.exp(m - best) for m, t in zip(tops, totals)]
    whole = functools.reduce(jnp.add, parts)
    latent_out = functools.reduce(
        jnp.add, [landed[s].astype(jnp.float32) * (parts[s] / whole) for s in range(DEVS)]
    ).astype(jnp.bfloat16)
    loads[3].wait()
    expanded = jnp.concatenate(
        [
            jnp.dot(
                latent_out[head * rows : (head + 1) * rows],
                expand[head],
                preferred_element_type=jnp.float32,
            ).astype(jnp.bfloat16)
            for head in range(heads)
        ],
        axis=1,
    )
    loads[4].wait()
    half = out.shape[1] // 2
    pieces = y_send.shape[1]
    wide = half // pieces
    for c in range(pieces):
        low = jnp.dot(expanded, weight[:, pl.ds(c * wide, wide)], preferred_element_type=jnp.float32)
        high = jnp.dot(
            expanded, weight[:, pl.ds(half + c * wide, wide)], preferred_element_type=jnp.float32
        )
        for step in (3, 2, 1, 0):
            both = jnp.concatenate(
                [low[step * own : (step + 1) * own], high[step * own : (step + 1) * own]], axis=0
            )
            mixed[step, :, pl.ds(c * wide, wide)] = both.astype(jnp.bfloat16)
            if step:
                launch(
                    remote(
                        mixed.at[step, :, pl.ds(c * wide, wide)],
                        landed_mixed.at[step, :, pl.ds(c * wide, wide)],
                        y_send.at[step, c],
                        y_recv.at[step, c],
                        step,
                    )
                )
    for c in range(pieces):
        both = mixed[0, :, pl.ds(c * wide, wide)].astype(jnp.float32)
        for step in (1, 2, 3):
            remote(
                mixed.at[step, :, pl.ds(c * wide, wide)],
                landed_mixed.at[step, :, pl.ds(c * wide, wide)],
                y_send.at[step, c],
                y_recv.at[step, c],
                step,
            ).wait_recv()
            both = both + landed_mixed[step, :, pl.ds(c * wide, wide)].astype(jnp.float32)
        out[:, pl.ds(c * wide, wide)] = both[0:own].astype(jnp.bfloat16)
        out[:, pl.ds(half + c * wide, wide)] = both[own : 2 * own].astype(jnp.bfloat16)
    for copy in sent:
        copy.wait_send()


def still_shards(
    queries,
    new_latents,
    prompt_blocks,
    block_routes,
    prompt_lengths,
    resident_blocks,
    resident_slots,
    key_absorb,
    value_expand,
    output_weight,
):
    requests, steps, all_heads, width = queries.shape
    heads = key_absorb.shape[0]
    lat = prompt_blocks.shape[2]
    prompt_rows = prompt_blocks.shape[0] * prompt_blocks.shape[1]
    home_rows = resident_blocks.shape[0] * resident_blocks.shape[1]
    total_rows = prompt_rows + home_rows + 128
    own = requests * steps
    rows = DEVS * own
    span = heads * rows
    rank = key_absorb.shape[2]
    model = output_weight.shape[1]
    pieces = 4
    by_head = (
        queries.reshape(own, DEVS, heads, width).transpose(1, 2, 0, 3).reshape(DEVS, heads * own, width)
    )
    smem = pl.BlockSpec(memory_space=pltpu.SMEM)
    vmem = pl.BlockSpec(memory_space=pltpu.VMEM)
    held = pl.BlockSpec(memory_space=pl.ANY)
    pair = pltpu.SemaphoreType.DMA((DEVS,))
    bf16 = jnp.bfloat16
    return pl.pallas_call(
        functools.partial(still_kernel, scale=1.0 / math.sqrt(width)),
        out_shape=jax.ShapeDtypeStruct((own, model), bf16),
        in_specs=[smem, smem, smem, vmem, vmem, held, held, held, held, held],
        out_specs=vmem,
        scratch_shapes=[
            pltpu.VMEM((total_rows, lat), bf16),
            pltpu.VMEM(key_absorb.shape, bf16),
            pltpu.VMEM(value_expand.shape, bf16),
            pltpu.VMEM(output_weight.shape, bf16),
            pltpu.VMEM((DEVS, heads * own, width), bf16),
            pltpu.VMEM((DEVS, own, 128), jnp.int32),
            pltpu.VMEM((DEVS, span, lat), bf16),
            pltpu.VMEM((rows, total_rows), jnp.float32),
            pltpu.VMEM((span, total_rows), jnp.float32),
            pltpu.VMEM((DEVS, span, rank), bf16),
            pltpu.VMEM((DEVS, 16, span), jnp.float32),
            pltpu.VMEM((DEVS, span, rank), bf16),
            pltpu.VMEM((DEVS, 16, span), jnp.float32),
            pltpu.VMEM((DEVS, 2 * own, model // 2), bf16),
            pltpu.VMEM((DEVS, 2 * own, model // 2), bf16),
            pltpu.SemaphoreType.DMA((5,)),
            pair,
            pair,
            pair,
            pair,
            pair,
            pair,
            pair,
            pair,
            pair,
            pair,
            pltpu.SemaphoreType.DMA((DEVS, pieces)),
            pltpu.SemaphoreType.DMA((DEVS, pieces)),
        ],
        compiler_params=pltpu.CompilerParams(
            collective_id=0, has_side_effects=True, vmem_limit_bytes=48 * 1024 * 1024
        ),
        name="still_attention",
    )(
        block_routes.reshape(-1),
        resident_slots,
        prompt_lengths,
        by_head,
        new_latents.reshape(own, lat),
        prompt_blocks.reshape(prompt_rows, lat),
        resident_blocks.reshape(home_rows, lat),
        key_absorb,
        value_expand,
        output_weight,
    )


def solution(mesh):
    body = still_shards if mesh.shape["dev"] == DEVS else routed_shards
    in_specs = (
        P(("groups", "dev", "pd"), None, None, None),
        P(("groups", "dev", "pd"), None, None),
        P(("groups", "dev", "pd"), None, None),
        P(("groups", "dev", "pd"), None),
        P(("groups", "dev", "pd")),
        P(("groups", "dev", "pd"), None, None),
        P(("groups", "dev", "pd")),
        P("dev", None, None),
        P("dev", None, None),
        P("dev", None),
    )
    out_specs = P(("groups", "dev", "pd"), None)
    return jax.shard_map(body, mesh=mesh, in_specs=in_specs, out_specs=out_specs, check_vma=False)
```

```python
import functools
import math

import jax
import jax.numpy as jnp
from jax import lax
from jax.experimental import pallas as pl
from jax.experimental.pallas import tpu as pltpu
from jax.sharding import PartitionSpec as P

KVR = 512


def deliver(prompt_blocks, block_routes, prompt_lengths):
    devices = lax.axis_size("dev")
    held = prompt_blocks.shape[0]
    width = prompt_blocks.shape[1]
    per_pair = max(1, 2 * held // devices)
    places = devices * per_pair
    destination = block_routes[:, 0]
    mine = (destination[:, None] == jnp.arange(devices, dtype=jnp.int32)[None, :]).astype(jnp.int32)
    rank = jnp.sum((jnp.cumsum(mine, axis=0) - mine) * mine, axis=1)
    position = destination * per_pair + rank
    select = jnp.arange(places, dtype=jnp.int32)[:, None] == position[None, :]
    outgoing = jnp.einsum(
        "sp,pbc->sbc",
        select.astype(jnp.bfloat16),
        prompt_blocks,
        preferred_element_type=jnp.float32,
    ).astype(jnp.bfloat16)
    marks = jnp.concatenate([jnp.ones((held, 1), jnp.int32), block_routes[:, 1:3]], axis=1)
    labels = jnp.sum(select.astype(jnp.int32)[:, :, None] * marks[None, :, :], axis=1)
    arrived, tags = (
        lax.all_to_all(
            outgoing.reshape(devices, per_pair, width, -1),
            "dev",
            split_axis=0,
            concat_axis=0,
            tiled=True,
        ),
        lax.all_to_all(
            labels.reshape(devices, per_pair, 3), "dev", split_axis=0, concat_axis=0, tiled=True
        ),
    )
    arrived = arrived.reshape(places, width, -1)
    tags = tags.reshape(places, 3)
    owners = tags[:, 1]
    requests = prompt_lengths.shape[0]
    lengths = jnp.sum(
        jnp.where(
            owners[:, None] == jnp.arange(requests, dtype=jnp.int32)[None, :],
            prompt_lengths[None, :],
            0,
        ),
        axis=1,
    )
    valid = tags[:, 0] * jnp.clip(lengths - width * tags[:, 2], 0, width)
    return (arrived, owners, valid)


def opening(queries, fresh, heads, scale):
    scores = jnp.einsum("rqc,rkc->rqk", queries, fresh, preferred_element_type=jnp.float32) * scale
    causal = jnp.arange(fresh.shape[1])[None, :] <= (jnp.arange(queries.shape[1]) // heads)[:, None]
    scores = jnp.where(causal[None], scores, -1e30)
    top = jnp.max(scores, axis=2)
    weight = jnp.where(causal[None], jnp.exp(scores - top[..., None]), 0.0)
    total = jnp.sum(weight, axis=2)
    carried = jnp.einsum(
        "rqk,rkc->rqc",
        weight.astype(jnp.bfloat16),
        fresh[..., :KVR],
        preferred_element_type=jnp.float32,
    )
    return (top, total, carried)


def sweep(state, queries, blocks, owners, valid, scale):
    count = blocks.shape[0]
    group = math.gcd(count, 8)
    rounds = count // group
    width = blocks.shape[1]
    requests = queries.shape[0]
    grouped = (
        blocks.reshape(rounds, group, width, blocks.shape[2]),
        owners.reshape(rounds, group),
        valid.reshape(rounds, group),
    )

    def advance(carry, piece):
        top, total, accum = carry
        block_keys, block_owner, block_valid = piece
        picked = jnp.take(queries, block_owner, axis=0)
        scores = (
            jnp.einsum("gqc,gkc->gqk", picked, block_keys, preferred_element_type=jnp.float32)
            * scale
        )
        live = jnp.arange(width)[None, :] < block_valid[:, None]
        scores = jnp.where(live[:, None, :], scores, -1e30)
        owned = block_owner[:, None] == jnp.arange(requests, dtype=jnp.int32)[None, :]
        best = jnp.max(
            jnp.where(owned[:, :, None], jnp.max(scores, axis=2)[:, None, :], -1e30), axis=0
        )
        new_top = jnp.maximum(top, best)
        weight = jnp.where(
            live[:, None, :],
            jnp.exp(scores - jnp.take(new_top, block_owner, axis=0)[:, :, None]),
            0.0,
        )
        ownf = owned.astype(jnp.float32)
        mass = jnp.einsum("gr,gq->rq", ownf, jnp.sum(weight, axis=2))
        carried = jnp.einsum(
            "gqk,gkc->gqc",
            weight.astype(jnp.bfloat16),
            block_keys[..., :KVR],
            preferred_element_type=jnp.float32,
        )
        factor = jnp.exp(top - new_top)
        total = total * factor + mass
        accum = accum * factor[..., None] + jnp.einsum("gr,gqc->rqc", ownf, carried)
        return ((new_top, total, accum), None)

    state, unused = lax.scan(advance, state, grouped)
    return state


def routed_shards(
    queries,
    new_latents,
    prompt_blocks,
    block_routes,
    prompt_lengths,
    resident_blocks,
    resident_slots,
    key_absorb,
    value_expand,
    output_weight,
):
    requests = queries.shape[0]
    steps = queries.shape[1]
    split_at = key_absorb.shape[1]
    scale = 1.0 / math.sqrt(queries.shape[3])
    piece = lax.all_to_all(queries, "dev", split_axis=2, concat_axis=0, tiled=True)
    latent = jnp.einsum(
        "rshn,hnc->rshc", piece[..., :split_at], key_absorb, preferred_element_type=jnp.float32
    ).astype(jnp.bfloat16)
    joined = jnp.concatenate([latent, piece[..., split_at:]], axis=-1)
    absorbed = lax.all_to_all(joined, "dev", split_axis=0, concat_axis=2, tiled=True)
    heads = absorbed.shape[2]
    flat_queries = absorbed.reshape(requests, steps * heads, absorbed.shape[3])
    state = opening(flat_queries, new_latents, heads, scale)
    home_valid = jnp.full((resident_blocks.shape[0],), resident_blocks.shape[1], jnp.int32)
    arrived, owners, valid = deliver(prompt_blocks, block_routes, prompt_lengths)
    joined_blocks = jnp.concatenate([resident_blocks, arrived], axis=0)
    joined_owners = jnp.concatenate([resident_slots, owners], axis=0)
    joined_valid = jnp.concatenate([home_valid, valid], axis=0)
    state = sweep(state, flat_queries, joined_blocks, joined_owners, joined_valid, scale)
    top, total, accum = state
    latent_out = (accum / total[..., None]).astype(jnp.bfloat16).reshape(requests, steps, heads, -1)
    expanded = jnp.einsum(
        "rshc,hcv->rshv",
        lax.all_to_all(latent_out, "dev", split_axis=2, concat_axis=0, tiled=True),
        value_expand,
        preferred_element_type=jnp.float32,
    ).astype(jnp.bfloat16)
    flat = expanded.reshape(expanded.shape[0] * steps, -1)
    mixed = lax.psum_scatter(
        jnp.dot(flat, output_weight, preferred_element_type=jnp.float32).astype(jnp.bfloat16),
        "dev",
        scatter_dimension=0,
        tiled=True,
    )
    return mixed


DEVS = 4
CHUNK = 1024
FAR = -1e30
MESH = pl.DeviceIdType.MESH


def partner(me, step):
    return (me, me + 1 - 2 * (me % 2), (me + 2) % 4, 3 - me)[step]


def still_kernel(
    routes,
    slots,
    lengths,
    queries_hbm,
    fresh_hbm,
    prompt_hbm,
    resident_hbm,
    absorb_hbm,
    expand_hbm,
    output_hbm,
    out,
    queries,
    spread,
    spread_rope,
    by_head,
    fresh,
    keys,
    absorb,
    expand,
    weight,
    asked,
    lens,
    absorbed,
    bias,
    scores,
    partial,
    stats,
    landed,
    landed_stats,
    mixed,
    landed_mixed,
    local_sem,
    block_sem,
    q_send,
    q_recv,
    n_send,
    n_recv,
    a_send,
    a_recv,
    o_send,
    o_recv,
    t_send,
    t_recv,
    y_send,
    y_recv,
    *,
    scale,
):
    me = lax.axis_index("dev")
    held, lat, block = prompt_hbm.shape
    homes = resident_hbm.shape[0]
    prompt_rows = held * block
    home_rows = homes * block
    heads, nope, rank = absorb.shape
    requests, steps, all_heads, width = queries.shape
    own = requests * steps
    new_rows = own
    rows = DEVS * own
    span = heads * rows

    loads = [
        pltpu.make_async_copy(queries_hbm, queries, local_sem.at[0]),
        pltpu.make_async_copy(absorb_hbm, absorb, local_sem.at[1]),
        pltpu.make_async_copy(fresh_hbm, fresh, local_sem.at[2]),
        pltpu.make_async_copy(expand_hbm, expand, local_sem.at[3]),
        pltpu.make_async_copy(output_hbm, weight, local_sem.at[4]),
    ]
    blocks = [
        pltpu.make_async_copy(source.at[b], keys.at[:, pl.ds((first + b) * block, block)], block_sem.at[first + b])
        for source, count, first in ((prompt_hbm, held, 0), (resident_hbm, homes, held))
        for b in range(count)
    ]
    for load in loads[:3] + blocks + loads[3:]:
        load.start()

    barrier = pltpu.get_barrier_semaphore()
    for step in range(1, DEVS):
        pl.semaphore_signal(barrier, inc=1, device_id={"dev": partner(me, step)}, device_id_type=MESH)
    pl.semaphore_wait(barrier, DEVS - 1)

    def remote(source, target, send, recv, step):
        return pltpu.make_async_remote_copy(
            src_ref=source,
            dst_ref=target,
            send_sem=send,
            recv_sem=recv,
            device_id={"dev": partner(me, step)},
            device_id_type=MESH,
        )

    sent = []

    def launch(copy):
        copy.start()
        sent.append(copy)
        return copy

    loads[0].wait()
    for r in range(own):
        rows_now = queries[r // steps, r % steps].astype(jnp.float32)
        for ref, at in ((spread, 0), (spread_rope, nope)):
            part = rows_now[:, at : at + nope]
            if part.shape[1] < nope:
                part = jnp.concatenate([part, jnp.zeros((all_heads, nope - part.shape[1]), jnp.float32)], axis=1)
            ref[pl.ds(r, all_heads, stride=own), :] = part
    by_head[:, :, 0:nope] = spread[...].astype(jnp.bfloat16).reshape(DEVS, heads * own, nope)
    by_head[:, :, nope:width] = (
        spread_rope[:, 0 : width - nope].astype(jnp.bfloat16).reshape(DEVS, heads * own, width - nope)
    )
    asks = {}
    for step in (3, 2, 1):
        asks[step] = launch(
            remote(by_head.at[partner(me, step)], asked.at[step], q_send.at[step], q_recv.at[step], step)
        )
    request_row = lax.broadcasted_iota(jnp.int32, (own, 128), 0) // steps
    length_rows = jnp.zeros((own, 128), jnp.int32)
    for r in range(requests):
        length_rows = jnp.where(request_row == r, lengths[r], length_rows)
    lens[0] = length_rows
    counts = {}
    for step in (3, 2, 1):
        counts[step] = launch(remote(lens.at[0], lens.at[step], n_send.at[step], n_recv.at[step], step))

    asked[0] = by_head[me]
    loads[2].wait()
    newest = [fresh[r].astype(jnp.float32) for r in range(requests)]
    padding = jnp.zeros((block - new_rows, lat), jnp.float32)
    newest = jnp.concatenate(newest + [padding], axis=0)
    keys[:, pl.ds(prompt_rows + home_rows, block)] = jnp.transpose(newest).astype(keys.dtype)

    for step in (1, 2, 3):
        asks[step].wait_recv()
    loads[1].wait()
    asking = [asked[step].astype(jnp.float32) for step in range(DEVS)]
    for head in range(heads):
        piece = jnp.concatenate([a[head * own : (head + 1) * own] for a in asking], axis=0).astype(
            jnp.bfloat16
        )
        latent = jnp.dot(piece[:, :nope], absorb[head], preferred_element_type=jnp.float32)
        absorbed[0, pl.ds(head * rows, rows), 0:rank] = latent.astype(jnp.bfloat16)
        absorbed[0, pl.ds(head * rows, rows), rank:lat] = piece[:, nope:]
    shares = {}
    for step in (1, 3, 2):
        shares[step] = launch(
            remote(absorbed.at[0], absorbed.at[step], a_send.at[step], a_recv.at[step], step)
        )

    for step in (1, 2, 3):
        counts[step].wait_recv()
    lane = lax.broadcasted_iota(jnp.int32, (rows, block), 1)
    row = lax.broadcasted_iota(jnp.int32, (rows, block), 0)
    row_length = jnp.concatenate([lens[step] for step in range(DEVS)], axis=0)
    row_device = jnp.zeros((rows, block), jnp.int32)
    for step in range(DEVS):
        row_device = jnp.where(row // own == step, partner(me, step), row_device)
    row_request = row_device * requests + (row % own) // steps
    for b in range(prompt_rows // block):
        owner = routes[0, b] * requests + routes[1, b]
        seen = (row_request == owner) & (routes[2, b] * block + lane < row_length)
        bias[:, pl.ds(b * block, block)] = jnp.where(seen, 0.0, FAR)
    for b in range(home_rows // block):
        seen = row_request == me * requests + slots[b]
        bias[:, pl.ds(prompt_rows + b * block, block)] = jnp.where(seen, 0.0, FAR)
    seen = (
        (row_request == me * requests + lane // steps)
        & (lane % steps <= row % steps)
        & (lane < new_rows)
    )
    total_rows = prompt_rows + home_rows + block
    bias[:, pl.ds(prompt_rows + home_rows, block)] = jnp.where(seen, 0.0, FAR)
    for load in blocks:
        load.wait()

    cuts = [(at, min(CHUNK, total_rows - at)) for at in range(0, total_rows, CHUNK)]
    for step in (0, 1, 3, 2):
        if step:
            shares[step].wait_recv()
        shard = absorbed[step]
        top = jnp.full((span, 1), FAR, jnp.float32)
        order = [s ^ step for s in range(DEVS)]
        for at, size in cuts:
            piece = jnp.dot(shard, keys[:, pl.ds(at, size)], preferred_element_type=jnp.float32)
            mask = jnp.concatenate(
                [bias[s * own : (s + 1) * own, at : at + size] for s in order], axis=0
            )
            piece = (piece * scale).reshape(heads, rows, size) + mask[None]
            piece = piece.reshape(span, size)
            scores[:, pl.ds(at, size)] = piece
            top = jnp.maximum(top, jnp.max(piece, axis=1, keepdims=True))
        total = jnp.zeros((span, 1), jnp.float32)
        summed = jnp.zeros((span, rank), jnp.float32)
        for at, size in cuts:
            live = jnp.exp(scores[:, pl.ds(at, size)] - top)
            total = total + jnp.sum(live, axis=1, keepdims=True)
            summed = summed + lax.dot_general(
                live.astype(jnp.bfloat16),
                keys[0:rank, pl.ds(at, size)],
                (((1,), (1,)), ((), ())),
                preferred_element_type=jnp.float32,
            )
        result = (summed / total).astype(jnp.bfloat16)
        top_row = jnp.transpose(jnp.broadcast_to(top, (span, 128)))[0:8]
        total_row = jnp.transpose(jnp.broadcast_to(total, (span, 128)))[0:8]
        if step:
            partial[step] = result
            stats[step, 0:8, :] = top_row
            stats[step, 8:16, :] = total_row
            launch(remote(stats.at[step], landed_stats.at[step], t_send.at[step], t_recv.at[step], step))
            launch(remote(partial.at[step], landed.at[step], o_send.at[step], o_recv.at[step], step))
        else:
            landed[0] = result
            landed_stats[0, 0:8, :] = top_row
            landed_stats[0, 8:16, :] = total_row

    for step in (1, 3, 2):
        remote(stats.at[step], landed_stats.at[step], t_send.at[step], t_recv.at[step], step).wait_recv()
        remote(partial.at[step], landed.at[step], o_send.at[step], o_recv.at[step], step).wait_recv()
    tops = [
        jnp.transpose(jnp.broadcast_to(landed_stats[s, 0:1, :], (128, span)))[:, 0:1] for s in range(DEVS)
    ]
    totals = [
        jnp.transpose(jnp.broadcast_to(landed_stats[s, 8:9, :], (128, span)))[:, 0:1] for s in range(DEVS)
    ]
    best = functools.reduce(jnp.maximum, tops)
    parts = [t * jnp.exp(m - best) for m, t in zip(tops, totals)]
    whole = functools.reduce(jnp.add, parts)
    latent_out = functools.reduce(
        jnp.add, [landed[s].astype(jnp.float32) * (parts[s] / whole) for s in range(DEVS)]
    ).astype(jnp.bfloat16)
    loads[3].wait()
    expanded = jnp.concatenate(
        [
            jnp.dot(
                latent_out[head * rows : (head + 1) * rows],
                expand[head],
                preferred_element_type=jnp.float32,
            ).astype(jnp.bfloat16)
            for head in range(heads)
        ],
        axis=1,
    )
    loads[4].wait()
    half = out.shape[1] // 2
    pieces = y_send.shape[1]
    wide = half // pieces
    for c in range(pieces):
        low = jnp.dot(expanded, weight[:, pl.ds(c * wide, wide)], preferred_element_type=jnp.float32)
        high = jnp.dot(
            expanded, weight[:, pl.ds(half + c * wide, wide)], preferred_element_type=jnp.float32
        )
        for step in (3, 2, 1, 0):
            both = jnp.concatenate(
                [low[step * own : (step + 1) * own], high[step * own : (step + 1) * own]], axis=0
            )
            mixed[step, :, pl.ds(c * wide, wide)] = both.astype(jnp.bfloat16)
            if step:
                launch(
                    remote(
                        mixed.at[step, :, pl.ds(c * wide, wide)],
                        landed_mixed.at[step, :, pl.ds(c * wide, wide)],
                        y_send.at[step, c],
                        y_recv.at[step, c],
                        step,
                    )
                )
    for c in range(pieces):
        both = mixed[0, :, pl.ds(c * wide, wide)].astype(jnp.float32)
        for step in (1, 2, 3):
            remote(
                mixed.at[step, :, pl.ds(c * wide, wide)],
                landed_mixed.at[step, :, pl.ds(c * wide, wide)],
                y_send.at[step, c],
                y_recv.at[step, c],
                step,
            ).wait_recv()
            both = both + landed_mixed[step, :, pl.ds(c * wide, wide)].astype(jnp.float32)
        out[:, pl.ds(c * wide, wide)] = both[0:own].astype(jnp.bfloat16)
        out[:, pl.ds(half + c * wide, wide)] = both[own : 2 * own].astype(jnp.bfloat16)
    for copy in sent:
        copy.wait_send()


def still_shards(
    queries,
    new_latents,
    prompt_blocks,
    block_routes,
    prompt_lengths,
    resident_blocks,
    resident_slots,
    key_absorb,
    value_expand,
    output_weight,
):
    requests, steps, all_heads, width = queries.shape
    heads = key_absorb.shape[0]
    held, block, lat = prompt_blocks.shape
    blocks = held + resident_blocks.shape[0]
    total_rows = (blocks + 1) * block
    own = requests * steps
    rows = DEVS * own
    span = heads * rows
    rank = key_absorb.shape[2]
    model = output_weight.shape[1]
    pieces = 4
    smem = pl.BlockSpec(memory_space=pltpu.SMEM)
    vmem = pl.BlockSpec(memory_space=pltpu.VMEM)
    far = pl.BlockSpec(memory_space=pl.ANY)
    pair = pltpu.SemaphoreType.DMA((DEVS,))
    bf16 = jnp.bfloat16
    return pl.pallas_call(
        functools.partial(still_kernel, scale=1.0 / math.sqrt(width)),
        out_shape=jax.ShapeDtypeStruct((own, model), bf16),
        in_specs=[smem] * 3 + [far] * 7,
        out_specs=vmem,
        scratch_shapes=[
            pltpu.VMEM(queries.shape, bf16),
            pltpu.VMEM((own * all_heads, 128), jnp.float32),
            pltpu.VMEM((own * all_heads, 128), jnp.float32),
            pltpu.VMEM((DEVS, heads * own, width), bf16),
            pltpu.VMEM(new_latents.shape, bf16),
            pltpu.VMEM((lat, total_rows), bf16),
            pltpu.VMEM(key_absorb.shape, bf16),
            pltpu.VMEM(value_expand.shape, bf16),
            pltpu.VMEM(output_weight.shape, bf16),
            pltpu.VMEM((DEVS, heads * own, width), bf16),
            pltpu.VMEM((DEVS, own, 128), jnp.int32),
            pltpu.VMEM((DEVS, span, lat), bf16),
            pltpu.VMEM((rows, total_rows), jnp.float32),
            pltpu.VMEM((span, total_rows), jnp.float32),
            pltpu.VMEM((DEVS, span, rank), bf16),
            pltpu.VMEM((DEVS, 16, span), jnp.float32),
            pltpu.VMEM((DEVS, span, rank), bf16),
            pltpu.VMEM((DEVS, 16, span), jnp.float32),
            pltpu.VMEM((DEVS, 2 * own, model // 2), bf16),
            pltpu.VMEM((DEVS, 2 * own, model // 2), bf16),
            pltpu.SemaphoreType.DMA((5,)),
            pltpu.SemaphoreType.DMA((blocks,)),
            pair,
            pair,
            pair,
            pair,
            pair,
            pair,
            pair,
            pair,
            pair,
            pair,
            pltpu.SemaphoreType.DMA((DEVS, pieces)),
            pltpu.SemaphoreType.DMA((DEVS, pieces)),
        ],
        compiler_params=pltpu.CompilerParams(
            collective_id=0, has_side_effects=True, vmem_limit_bytes=63 * 1024 * 1024
        ),
        name="still_attention",
    )(
        block_routes.T,
        resident_slots,
        prompt_lengths,
        queries,
        new_latents,
        prompt_blocks.transpose(0, 2, 1),
        resident_blocks.transpose(0, 2, 1),
        key_absorb,
        value_expand,
        output_weight,
    )


def solution(mesh):
    body = still_shards if mesh.shape["dev"] == DEVS else routed_shards
    in_specs = (
        P(("groups", "dev", "pd"), None, None, None),
        P(("groups", "dev", "pd"), None, None),
        P(("groups", "dev", "pd"), None, None),
        P(("groups", "dev", "pd"), None),
        P(("groups", "dev", "pd")),
        P(("groups", "dev", "pd"), None, None),
        P(("groups", "dev", "pd")),
        P("dev", None, None),
        P("dev", None, None),
        P("dev", None),
    )
    out_specs = P(("groups", "dev", "pd"), None)
    return jax.shard_map(body, mesh=mesh, in_specs=in_specs, out_specs=out_specs, check_vma=False)
```

```python
import functools
import math

import jax
import jax.numpy as jnp
from jax import lax
from jax.experimental import pallas as pl
from jax.experimental.pallas import tpu as pltpu
from jax.sharding import PartitionSpec as P

KVR = 512


def deliver(prompt_blocks, block_routes, prompt_lengths):
    devices = lax.axis_size("dev")
    held = prompt_blocks.shape[0]
    width = prompt_blocks.shape[1]
    per_pair = max(1, 2 * held // devices)
    places = devices * per_pair
    destination = block_routes[:, 0]
    mine = (destination[:, None] == jnp.arange(devices, dtype=jnp.int32)[None, :]).astype(jnp.int32)
    rank = jnp.sum((jnp.cumsum(mine, axis=0) - mine) * mine, axis=1)
    position = destination * per_pair + rank
    select = jnp.arange(places, dtype=jnp.int32)[:, None] == position[None, :]
    outgoing = jnp.einsum(
        "sp,pbc->sbc",
        select.astype(jnp.bfloat16),
        prompt_blocks,
        preferred_element_type=jnp.float32,
    ).astype(jnp.bfloat16)
    marks = jnp.concatenate([jnp.ones((held, 1), jnp.int32), block_routes[:, 1:3]], axis=1)
    labels = jnp.sum(select.astype(jnp.int32)[:, :, None] * marks[None, :, :], axis=1)
    arrived, tags = (
        lax.all_to_all(
            outgoing.reshape(devices, per_pair, width, -1),
            "dev",
            split_axis=0,
            concat_axis=0,
            tiled=True,
        ),
        lax.all_to_all(
            labels.reshape(devices, per_pair, 3), "dev", split_axis=0, concat_axis=0, tiled=True
        ),
    )
    arrived = arrived.reshape(places, width, -1)
    tags = tags.reshape(places, 3)
    owners = tags[:, 1]
    requests = prompt_lengths.shape[0]
    lengths = jnp.sum(
        jnp.where(
            owners[:, None] == jnp.arange(requests, dtype=jnp.int32)[None, :],
            prompt_lengths[None, :],
            0,
        ),
        axis=1,
    )
    valid = tags[:, 0] * jnp.clip(lengths - width * tags[:, 2], 0, width)
    return (arrived, owners, valid)


def opening(queries, fresh, heads, scale):
    scores = jnp.einsum("rqc,rkc->rqk", queries, fresh, preferred_element_type=jnp.float32) * scale
    causal = jnp.arange(fresh.shape[1])[None, :] <= (jnp.arange(queries.shape[1]) // heads)[:, None]
    scores = jnp.where(causal[None], scores, -1e30)
    top = jnp.max(scores, axis=2)
    weight = jnp.where(causal[None], jnp.exp(scores - top[..., None]), 0.0)
    total = jnp.sum(weight, axis=2)
    carried = jnp.einsum(
        "rqk,rkc->rqc",
        weight.astype(jnp.bfloat16),
        fresh[..., :KVR],
        preferred_element_type=jnp.float32,
    )
    return (top, total, carried)


def sweep(state, queries, blocks, owners, valid, scale):
    count = blocks.shape[0]
    group = math.gcd(count, 8)
    rounds = count // group
    width = blocks.shape[1]
    requests = queries.shape[0]
    grouped = (
        blocks.reshape(rounds, group, width, blocks.shape[2]),
        owners.reshape(rounds, group),
        valid.reshape(rounds, group),
    )

    def advance(carry, piece):
        top, total, accum = carry
        block_keys, block_owner, block_valid = piece
        picked = jnp.take(queries, block_owner, axis=0)
        scores = (
            jnp.einsum("gqc,gkc->gqk", picked, block_keys, preferred_element_type=jnp.float32)
            * scale
        )
        live = jnp.arange(width)[None, :] < block_valid[:, None]
        scores = jnp.where(live[:, None, :], scores, -1e30)
        owned = block_owner[:, None] == jnp.arange(requests, dtype=jnp.int32)[None, :]
        best = jnp.max(
            jnp.where(owned[:, :, None], jnp.max(scores, axis=2)[:, None, :], -1e30), axis=0
        )
        new_top = jnp.maximum(top, best)
        weight = jnp.where(
            live[:, None, :],
            jnp.exp(scores - jnp.take(new_top, block_owner, axis=0)[:, :, None]),
            0.0,
        )
        ownf = owned.astype(jnp.float32)
        mass = jnp.einsum("gr,gq->rq", ownf, jnp.sum(weight, axis=2))
        carried = jnp.einsum(
            "gqk,gkc->gqc",
            weight.astype(jnp.bfloat16),
            block_keys[..., :KVR],
            preferred_element_type=jnp.float32,
        )
        factor = jnp.exp(top - new_top)
        total = total * factor + mass
        accum = accum * factor[..., None] + jnp.einsum("gr,gqc->rqc", ownf, carried)
        return ((new_top, total, accum), None)

    state, unused = lax.scan(advance, state, grouped)
    return state


def routed_shards(
    queries,
    new_latents,
    prompt_blocks,
    block_routes,
    prompt_lengths,
    resident_blocks,
    resident_slots,
    key_absorb,
    value_expand,
    output_weight,
):
    requests = queries.shape[0]
    steps = queries.shape[1]
    split_at = key_absorb.shape[1]
    scale = 1.0 / math.sqrt(queries.shape[3])
    piece = lax.all_to_all(queries, "dev", split_axis=2, concat_axis=0, tiled=True)
    latent = jnp.einsum(
        "rshn,hnc->rshc", piece[..., :split_at], key_absorb, preferred_element_type=jnp.float32
    ).astype(jnp.bfloat16)
    joined = jnp.concatenate([latent, piece[..., split_at:]], axis=-1)
    absorbed = lax.all_to_all(joined, "dev", split_axis=0, concat_axis=2, tiled=True)
    heads = absorbed.shape[2]
    flat_queries = absorbed.reshape(requests, steps * heads, absorbed.shape[3])
    state = opening(flat_queries, new_latents, heads, scale)
    home_valid = jnp.full((resident_blocks.shape[0],), resident_blocks.shape[1], jnp.int32)
    arrived, owners, valid = deliver(prompt_blocks, block_routes, prompt_lengths)
    joined_blocks = jnp.concatenate([resident_blocks, arrived], axis=0)
    joined_owners = jnp.concatenate([resident_slots, owners], axis=0)
    joined_valid = jnp.concatenate([home_valid, valid], axis=0)
    state = sweep(state, flat_queries, joined_blocks, joined_owners, joined_valid, scale)
    top, total, accum = state
    latent_out = (accum / total[..., None]).astype(jnp.bfloat16).reshape(requests, steps, heads, -1)
    expanded = jnp.einsum(
        "rshc,hcv->rshv",
        lax.all_to_all(latent_out, "dev", split_axis=2, concat_axis=0, tiled=True),
        value_expand,
        preferred_element_type=jnp.float32,
    ).astype(jnp.bfloat16)
    flat = expanded.reshape(expanded.shape[0] * steps, -1)
    mixed = lax.psum_scatter(
        jnp.dot(flat, output_weight, preferred_element_type=jnp.float32).astype(jnp.bfloat16),
        "dev",
        scatter_dimension=0,
        tiled=True,
    )
    return mixed


DEVS = 4
CHUNK = 1024
FAR = -1e30
MESH = pl.DeviceIdType.MESH


def partner(me, step):
    return (me, me + 1 - 2 * (me % 2), (me + 2) % 4, 3 - me)[step]


def still_kernel(
    routes,
    slots,
    lengths,
    queries_hbm,
    fresh_hbm,
    prompt_hbm,
    resident_hbm,
    absorb_hbm,
    expand_hbm,
    output_hbm,
    out,
    queries,
    spread,
    spread_rope,
    by_head,
    fresh,
    keys,
    absorb,
    expand,
    weight,
    ropes,
    asked,
    lens,
    absorbed,
    bias,
    scores,
    partial,
    stats,
    landed,
    landed_stats,
    mixed,
    landed_mixed,
    local_sem,
    block_sem,
    q_send,
    q_recv,
    n_send,
    n_recv,
    r_send,
    r_recv,
    a_send,
    a_recv,
    o_send,
    o_recv,
    t_send,
    t_recv,
    y_send,
    y_recv,
    *,
    scale,
):
    me = lax.axis_index("dev")
    held, lat, block = prompt_hbm.shape
    homes = resident_hbm.shape[0]
    prompt_rows = held * block
    home_rows = homes * block
    heads, nope, rank = absorb.shape
    requests, steps, all_heads, width = queries.shape
    own = requests * steps
    new_rows = own
    rows = DEVS * own
    span = heads * rows

    loads = [
        pltpu.make_async_copy(queries_hbm, queries, local_sem.at[0]),
        pltpu.make_async_copy(absorb_hbm, absorb, local_sem.at[1]),
        pltpu.make_async_copy(fresh_hbm, fresh, local_sem.at[2]),
        pltpu.make_async_copy(expand_hbm, expand, local_sem.at[3]),
        pltpu.make_async_copy(output_hbm, weight, local_sem.at[4]),
    ]
    blocks = [
        pltpu.make_async_copy(source.at[b], keys.at[:, pl.ds((first + b) * block, block)], block_sem.at[first + b])
        for source, count, first in ((prompt_hbm, held, 0), (resident_hbm, homes, held))
        for b in range(count)
    ]
    for load in loads[:3] + blocks + loads[3:]:
        load.start()

    barrier = pltpu.get_barrier_semaphore()
    for step in range(1, DEVS):
        pl.semaphore_signal(barrier, inc=1, device_id={"dev": partner(me, step)}, device_id_type=MESH)
    pl.semaphore_wait(barrier, DEVS - 1)

    def remote(source, target, send, recv, step):
        return pltpu.make_async_remote_copy(
            src_ref=source,
            dst_ref=target,
            send_sem=send,
            recv_sem=recv,
            device_id={"dev": partner(me, step)},
            device_id_type=MESH,
        )

    sent = []

    def launch(copy):
        copy.start()
        sent.append(copy)
        return copy

    loads[0].wait()
    for r in range(own):
        rows_now = queries[r // steps, r % steps].astype(jnp.float32)
        for ref, at in ((spread, 0), (spread_rope, nope)):
            part = rows_now[:, at : at + nope]
            if part.shape[1] < nope:
                part = jnp.concatenate([part, jnp.zeros((all_heads, nope - part.shape[1]), jnp.float32)], axis=1)
            ref[pl.ds(r, all_heads, stride=own), :] = part
    by_head[...] = spread[...].astype(jnp.bfloat16).reshape(by_head.shape)
    turned = spread_rope[:, 0 : width - nope].reshape(DEVS, heads * own, width - nope)
    middle = heads * own // 2
    ropes[0] = jnp.concatenate([turned[:, :middle], turned[:, middle:]], axis=2).astype(jnp.bfloat16)
    asks = {}
    for step in (3, 2, 1):
        asks[step] = launch(
            remote(by_head.at[partner(me, step)], asked.at[step], q_send.at[step], q_recv.at[step], step)
        )
    request_row = lax.broadcasted_iota(jnp.int32, (own, 128), 0) // steps
    length_rows = jnp.zeros((own, 128), jnp.int32)
    for r in range(requests):
        length_rows = jnp.where(request_row == r, lengths[r], length_rows)
    lens[0] = length_rows
    counts = {}
    rotary = {}
    for step in (3, 2, 1):
        rotary[step] = launch(remote(ropes.at[0], ropes.at[step], r_send.at[step], r_recv.at[step], step))
    for step in (3, 2, 1):
        counts[step] = launch(remote(lens.at[0], lens.at[step], n_send.at[step], n_recv.at[step], step))

    asked[0] = by_head[me]
    loads[2].wait()
    newest = [fresh[r].astype(jnp.float32) for r in range(requests)]
    padding = jnp.zeros((block - new_rows, lat), jnp.float32)
    newest = jnp.concatenate(newest + [padding], axis=0)
    keys[:, pl.ds(prompt_rows + home_rows, block)] = jnp.transpose(newest).astype(keys.dtype)

    for step in (1, 2, 3):
        asks[step].wait_recv()
    loads[1].wait()
    asking = [asked[step].astype(jnp.float32) for step in range(DEVS)]
    for head in range(heads):
        piece = jnp.concatenate([a[head * own : (head + 1) * own] for a in asking], axis=0).astype(
            jnp.bfloat16
        )
        latent = jnp.dot(piece, absorb[head], preferred_element_type=jnp.float32)
        absorbed[0, pl.ds(head * rows, rows), :] = latent.astype(jnp.bfloat16)
    shares = {}
    for step in (2, 1):
        for part in range(2):
            at = pl.ds(part * (span // 2), span // 2)
            shares[step, part] = launch(
                remote(absorbed.at[0, at], absorbed.at[step, at], a_send.at[step, part], a_recv.at[step, part], step)
            )

    def hand_on(part):
        at = pl.ds(part * (span // 2), span // 2)
        shares[2, part].wait_recv()
        shares[3, part] = launch(
            remote(absorbed.at[2, at], absorbed.at[3, at], a_send.at[3, part], a_recv.at[3, part], 1)
        )

    for step in (1, 2, 3):
        counts[step].wait_recv()
        rotary[step].wait_recv()
    lane = lax.broadcasted_iota(jnp.int32, (rows, block), 1)
    row = lax.broadcasted_iota(jnp.int32, (rows, block), 0)
    row_length = jnp.concatenate([lens[step] for step in range(DEVS)], axis=0)
    row_device = jnp.zeros((rows, block), jnp.int32)
    for step in range(DEVS):
        row_device = jnp.where(row // own == step, partner(me, step), row_device)
    row_request = row_device * requests + (row % own) // steps
    for b in range(prompt_rows // block):
        owner = routes[0, b] * requests + routes[1, b]
        seen = (row_request == owner) & (routes[2, b] * block + lane < row_length)
        bias[:, pl.ds(b * block, block)] = jnp.where(seen, 0.0, FAR)
    for b in range(home_rows // block):
        seen = row_request == me * requests + slots[b]
        bias[:, pl.ds(prompt_rows + b * block, block)] = jnp.where(seen, 0.0, FAR)
    seen = (
        (row_request == me * requests + lane // steps)
        & (lane % steps <= row % steps)
        & (lane < new_rows)
    )
    total_rows = prompt_rows + home_rows + block
    bias[:, pl.ds(prompt_rows + home_rows, block)] = jnp.where(seen, 0.0, FAR)
    for load in blocks:
        load.wait()

    cuts = [(at, min(CHUNK, total_rows - at)) for at in range(0, total_rows, CHUNK)]
    for step in range(DEVS):
        if step == 1:
            hand_on(0)
        if step == 2:
            hand_on(1)
        if step in (1, 3):
            for part in range(2):
                shares[step, part].wait_recv()
        holder = partner(me, step)
        order = [s ^ step for s in range(DEVS)]
        turned = []
        for s in order:
            packed = ropes[s, holder].astype(jnp.float32)
            turned.append(jnp.concatenate([packed[:, : width - nope], packed[:, width - nope :]], axis=0))
        turned = jnp.concatenate(
            [a[head * own : (head + 1) * own] for head in range(heads) for a in turned], axis=0
        ).astype(jnp.bfloat16)
        shard = jnp.concatenate([absorbed[step], turned], axis=1)
        top = jnp.full((span, 1), FAR, jnp.float32)
        for at, size in cuts:
            piece = jnp.dot(shard, keys[:, pl.ds(at, size)], preferred_element_type=jnp.float32)
            mask = jnp.concatenate(
                [bias[s * own : (s + 1) * own, at : at + size] for s in order], axis=0
            )
            piece = (piece * scale).reshape(heads, rows, size) + mask[None]
            piece = piece.reshape(span, size)
            scores[:, pl.ds(at, size)] = piece
            top = jnp.maximum(top, jnp.max(piece, axis=1, keepdims=True))
        total = jnp.zeros((span, 1), jnp.float32)
        summed = jnp.zeros((span, rank), jnp.float32)
        for at, size in cuts:
            live = jnp.exp(scores[:, pl.ds(at, size)] - top)
            total = total + jnp.sum(live, axis=1, keepdims=True)
            summed = summed + lax.dot_general(
                live.astype(jnp.bfloat16),
                keys[0:rank, pl.ds(at, size)],
                (((1,), (1,)), ((), ())),
                preferred_element_type=jnp.float32,
            )
        result = (summed / total).astype(jnp.bfloat16)
        top_row = jnp.transpose(jnp.broadcast_to(top, (span, 128)))[0:8]
        total_row = jnp.transpose(jnp.broadcast_to(total, (span, 128)))[0:8]
        if step:
            partial[step] = result
            stats[step, 0:8, :] = top_row
            stats[step, 8:16, :] = total_row
            launch(remote(stats.at[step], landed_stats.at[step], t_send.at[step], t_recv.at[step], step))
            launch(remote(partial.at[step], landed.at[step], o_send.at[step], o_recv.at[step], step))
        else:
            landed[0] = result
            landed_stats[0, 0:8, :] = top_row
            landed_stats[0, 8:16, :] = total_row

    for step in (1, 3, 2):
        remote(stats.at[step], landed_stats.at[step], t_send.at[step], t_recv.at[step], step).wait_recv()
        remote(partial.at[step], landed.at[step], o_send.at[step], o_recv.at[step], step).wait_recv()
    tops = [
        jnp.transpose(jnp.broadcast_to(landed_stats[s, 0:1, :], (128, span)))[:, 0:1] for s in range(DEVS)
    ]
    totals = [
        jnp.transpose(jnp.broadcast_to(landed_stats[s, 8:9, :], (128, span)))[:, 0:1] for s in range(DEVS)
    ]
    best = functools.reduce(jnp.maximum, tops)
    parts = [t * jnp.exp(m - best) for m, t in zip(tops, totals)]
    whole = functools.reduce(jnp.add, parts)
    latent_out = functools.reduce(
        jnp.add, [landed[s].astype(jnp.float32) * (parts[s] / whole) for s in range(DEVS)]
    ).astype(jnp.bfloat16)
    loads[3].wait()
    expanded = jnp.concatenate(
        [
            jnp.dot(
                latent_out[head * rows : (head + 1) * rows],
                expand[head],
                preferred_element_type=jnp.float32,
            ).astype(jnp.bfloat16)
            for head in range(heads)
        ],
        axis=1,
    )
    loads[4].wait()
    half = out.shape[1] // 2
    pieces = y_send.shape[1]
    wide = half // pieces
    for c in range(pieces):
        low = jnp.dot(expanded, weight[:, pl.ds(c * wide, wide)], preferred_element_type=jnp.float32)
        high = jnp.dot(
            expanded, weight[:, pl.ds(half + c * wide, wide)], preferred_element_type=jnp.float32
        )
        for step in (3, 2, 1, 0):
            both = jnp.concatenate(
                [low[step * own : (step + 1) * own], high[step * own : (step + 1) * own]], axis=0
            )
            mixed[step, :, pl.ds(c * wide, wide)] = both.astype(jnp.bfloat16)
            if step:
                launch(
                    remote(
                        mixed.at[step, :, pl.ds(c * wide, wide)],
                        landed_mixed.at[step, :, pl.ds(c * wide, wide)],
                        y_send.at[step, c],
                        y_recv.at[step, c],
                        step,
                    )
                )
    for c in range(pieces):
        both = mixed[0, :, pl.ds(c * wide, wide)].astype(jnp.float32)
        for step in (1, 2, 3):
            remote(
                mixed.at[step, :, pl.ds(c * wide, wide)],
                landed_mixed.at[step, :, pl.ds(c * wide, wide)],
                y_send.at[step, c],
                y_recv.at[step, c],
                step,
            ).wait_recv()
            both = both + landed_mixed[step, :, pl.ds(c * wide, wide)].astype(jnp.float32)
        out[:, pl.ds(c * wide, wide)] = both[0:own].astype(jnp.bfloat16)
        out[:, pl.ds(half + c * wide, wide)] = both[own : 2 * own].astype(jnp.bfloat16)
    for copy in sent:
        copy.wait_send()


def still_shards(
    queries,
    new_latents,
    prompt_blocks,
    block_routes,
    prompt_lengths,
    resident_blocks,
    resident_slots,
    key_absorb,
    value_expand,
    output_weight,
):
    requests, steps, all_heads, width = queries.shape
    heads = key_absorb.shape[0]
    held, block, lat = prompt_blocks.shape
    blocks = held + resident_blocks.shape[0]
    total_rows = (blocks + 1) * block
    own = requests * steps
    rows = DEVS * own
    span = heads * rows
    rank = key_absorb.shape[2]
    model = output_weight.shape[1]
    pieces = 4
    smem = pl.BlockSpec(memory_space=pltpu.SMEM)
    vmem = pl.BlockSpec(memory_space=pltpu.VMEM)
    far = pl.BlockSpec(memory_space=pl.ANY)
    pair = pltpu.SemaphoreType.DMA((DEVS,))
    halves = pltpu.SemaphoreType.DMA((DEVS, 2))
    bf16 = jnp.bfloat16
    return pl.pallas_call(
        functools.partial(still_kernel, scale=1.0 / math.sqrt(width)),
        out_shape=jax.ShapeDtypeStruct((own, model), bf16),
        in_specs=[smem] * 3 + [far] * 7,
        out_specs=vmem,
        scratch_shapes=[
            pltpu.VMEM(queries.shape, bf16),
            pltpu.VMEM((own * all_heads, 128), jnp.float32),
            pltpu.VMEM((own * all_heads, 128), jnp.float32),
            pltpu.VMEM((DEVS, heads * own, key_absorb.shape[1]), bf16),
            pltpu.VMEM(new_latents.shape, bf16),
            pltpu.VMEM((lat, total_rows), bf16),
            pltpu.VMEM(key_absorb.shape, bf16),
            pltpu.VMEM(value_expand.shape, bf16),
            pltpu.VMEM(output_weight.shape, bf16),
            pltpu.VMEM((DEVS, DEVS, heads * own // 2, 2 * (width - key_absorb.shape[1])), bf16),
            pltpu.VMEM((DEVS, heads * own, key_absorb.shape[1]), bf16),
            pltpu.VMEM((DEVS, own, 128), jnp.int32),
            pltpu.VMEM((DEVS, span, rank), bf16),
            pltpu.VMEM((rows, total_rows), jnp.float32),
            pltpu.VMEM((span, total_rows), jnp.float32),
            pltpu.VMEM((DEVS, span, rank), bf16),
            pltpu.VMEM((DEVS, 16, span), jnp.float32),
            pltpu.VMEM((DEVS, span, rank), bf16),
            pltpu.VMEM((DEVS, 16, span), jnp.float32),
            pltpu.VMEM((DEVS, 2 * own, model // 2), bf16),
            pltpu.VMEM((DEVS, 2 * own, model // 2), bf16),
            pltpu.SemaphoreType.DMA((5,)),
            pltpu.SemaphoreType.DMA((blocks,)),
            pair,
            pair,
            pair,
            pair,
            pair,
            pair,
            halves,
            halves,
            pair,
            pair,
            pair,
            pair,
            pltpu.SemaphoreType.DMA((DEVS, pieces)),
            pltpu.SemaphoreType.DMA((DEVS, pieces)),
        ],
        compiler_params=pltpu.CompilerParams(
            collective_id=0, has_side_effects=True, vmem_limit_bytes=63 * 1024 * 1024
        ),
        name="still_attention",
    )(
        block_routes.T,
        resident_slots,
        prompt_lengths,
        queries,
        new_latents,
        prompt_blocks.transpose(0, 2, 1),
        resident_blocks.transpose(0, 2, 1),
        key_absorb,
        value_expand,
        output_weight,
    )


def solution(mesh):
    body = still_shards if mesh.shape["dev"] == DEVS else routed_shards
    in_specs = (
        P(("groups", "dev", "pd"), None, None, None),
        P(("groups", "dev", "pd"), None, None),
        P(("groups", "dev", "pd"), None, None),
        P(("groups", "dev", "pd"), None),
        P(("groups", "dev", "pd")),
        P(("groups", "dev", "pd"), None, None),
        P(("groups", "dev", "pd")),
        P("dev", None, None),
        P("dev", None, None),
        P("dev", None),
    )
    out_specs = P(("groups", "dev", "pd"), None)
    return jax.shard_map(body, mesh=mesh, in_specs=in_specs, out_specs=out_specs, check_vma=False)
```

```python
import functools
import math

import jax
import jax.numpy as jnp
from jax import lax
from jax.experimental import pallas as pl
from jax.experimental.pallas import tpu as pltpu
from jax.sharding import PartitionSpec as P

KVR = 512


def deliver(prompt_blocks, block_routes, prompt_lengths):
    devices = lax.axis_size("dev")
    held = prompt_blocks.shape[0]
    width = prompt_blocks.shape[1]
    per_pair = max(1, 2 * held // devices)
    places = devices * per_pair
    destination = block_routes[:, 0]
    mine = (destination[:, None] == jnp.arange(devices, dtype=jnp.int32)[None, :]).astype(jnp.int32)
    rank = jnp.sum((jnp.cumsum(mine, axis=0) - mine) * mine, axis=1)
    position = destination * per_pair + rank
    select = jnp.arange(places, dtype=jnp.int32)[:, None] == position[None, :]
    outgoing = jnp.einsum(
        "sp,pbc->sbc",
        select.astype(jnp.bfloat16),
        prompt_blocks,
        preferred_element_type=jnp.float32,
    ).astype(jnp.bfloat16)
    marks = jnp.concatenate([jnp.ones((held, 1), jnp.int32), block_routes[:, 1:3]], axis=1)
    labels = jnp.sum(select.astype(jnp.int32)[:, :, None] * marks[None, :, :], axis=1)
    arrived, tags = (
        lax.all_to_all(
            outgoing.reshape(devices, per_pair, width, -1),
            "dev",
            split_axis=0,
            concat_axis=0,
            tiled=True,
        ),
        lax.all_to_all(
            labels.reshape(devices, per_pair, 3), "dev", split_axis=0, concat_axis=0, tiled=True
        ),
    )
    arrived = arrived.reshape(places, width, -1)
    tags = tags.reshape(places, 3)
    owners = tags[:, 1]
    requests = prompt_lengths.shape[0]
    lengths = jnp.sum(
        jnp.where(
            owners[:, None] == jnp.arange(requests, dtype=jnp.int32)[None, :],
            prompt_lengths[None, :],
            0,
        ),
        axis=1,
    )
    valid = tags[:, 0] * jnp.clip(lengths - width * tags[:, 2], 0, width)
    return (arrived, owners, valid)


def opening(queries, fresh, heads, scale):
    scores = jnp.einsum("rqc,rkc->rqk", queries, fresh, preferred_element_type=jnp.float32) * scale
    causal = jnp.arange(fresh.shape[1])[None, :] <= (jnp.arange(queries.shape[1]) // heads)[:, None]
    scores = jnp.where(causal[None], scores, -1e30)
    top = jnp.max(scores, axis=2)
    weight = jnp.where(causal[None], jnp.exp(scores - top[..., None]), 0.0)
    total = jnp.sum(weight, axis=2)
    carried = jnp.einsum(
        "rqk,rkc->rqc",
        weight.astype(jnp.bfloat16),
        fresh[..., :KVR],
        preferred_element_type=jnp.float32,
    )
    return (top, total, carried)


def sweep(state, queries, blocks, owners, valid, scale):
    count = blocks.shape[0]
    group = math.gcd(count, 8)
    rounds = count // group
    width = blocks.shape[1]
    requests = queries.shape[0]
    grouped = (
        blocks.reshape(rounds, group, width, blocks.shape[2]),
        owners.reshape(rounds, group),
        valid.reshape(rounds, group),
    )

    def advance(carry, piece):
        top, total, accum = carry
        block_keys, block_owner, block_valid = piece
        picked = jnp.take(queries, block_owner, axis=0)
        scores = (
            jnp.einsum("gqc,gkc->gqk", picked, block_keys, preferred_element_type=jnp.float32)
            * scale
        )
        live = jnp.arange(width)[None, :] < block_valid[:, None]
        scores = jnp.where(live[:, None, :], scores, -1e30)
        owned = block_owner[:, None] == jnp.arange(requests, dtype=jnp.int32)[None, :]
        best = jnp.max(
            jnp.where(owned[:, :, None], jnp.max(scores, axis=2)[:, None, :], -1e30), axis=0
        )
        new_top = jnp.maximum(top, best)
        weight = jnp.where(
            live[:, None, :],
            jnp.exp(scores - jnp.take(new_top, block_owner, axis=0)[:, :, None]),
            0.0,
        )
        ownf = owned.astype(jnp.float32)
        mass = jnp.einsum("gr,gq->rq", ownf, jnp.sum(weight, axis=2))
        carried = jnp.einsum(
            "gqk,gkc->gqc",
            weight.astype(jnp.bfloat16),
            block_keys[..., :KVR],
            preferred_element_type=jnp.float32,
        )
        factor = jnp.exp(top - new_top)
        total = total * factor + mass
        accum = accum * factor[..., None] + jnp.einsum("gr,gqc->rqc", ownf, carried)
        return ((new_top, total, accum), None)

    state, unused = lax.scan(advance, state, grouped)
    return state


def routed_shards(
    queries,
    new_latents,
    prompt_blocks,
    block_routes,
    prompt_lengths,
    resident_blocks,
    resident_slots,
    key_absorb,
    value_expand,
    output_weight,
):
    requests = queries.shape[0]
    steps = queries.shape[1]
    split_at = key_absorb.shape[1]
    scale = 1.0 / math.sqrt(queries.shape[3])
    piece = lax.all_to_all(queries, "dev", split_axis=2, concat_axis=0, tiled=True)
    latent = jnp.einsum(
        "rshn,hnc->rshc", piece[..., :split_at], key_absorb, preferred_element_type=jnp.float32
    ).astype(jnp.bfloat16)
    joined = jnp.concatenate([latent, piece[..., split_at:]], axis=-1)
    absorbed = lax.all_to_all(joined, "dev", split_axis=0, concat_axis=2, tiled=True)
    heads = absorbed.shape[2]
    flat_queries = absorbed.reshape(requests, steps * heads, absorbed.shape[3])
    state = opening(flat_queries, new_latents, heads, scale)
    home_valid = jnp.full((resident_blocks.shape[0],), resident_blocks.shape[1], jnp.int32)
    arrived, owners, valid = deliver(prompt_blocks, block_routes, prompt_lengths)
    joined_blocks = jnp.concatenate([resident_blocks, arrived], axis=0)
    joined_owners = jnp.concatenate([resident_slots, owners], axis=0)
    joined_valid = jnp.concatenate([home_valid, valid], axis=0)
    state = sweep(state, flat_queries, joined_blocks, joined_owners, joined_valid, scale)
    top, total, accum = state
    latent_out = (accum / total[..., None]).astype(jnp.bfloat16).reshape(requests, steps, heads, -1)
    expanded = jnp.einsum(
        "rshc,hcv->rshv",
        lax.all_to_all(latent_out, "dev", split_axis=2, concat_axis=0, tiled=True),
        value_expand,
        preferred_element_type=jnp.float32,
    ).astype(jnp.bfloat16)
    flat = expanded.reshape(expanded.shape[0] * steps, -1)
    mixed = lax.psum_scatter(
        jnp.dot(flat, output_weight, preferred_element_type=jnp.float32).astype(jnp.bfloat16),
        "dev",
        scatter_dimension=0,
        tiled=True,
    )
    return mixed


DEVS = 4
CHUNK = 1024
FAR = -1e30
MESH = pl.DeviceIdType.MESH


def partner(me, step):
    return (me, me + 1 - 2 * (me % 2), (me + 2) % 4, 3 - me)[step]


def still_kernel(
    routes,
    slots,
    lengths,
    queries_hbm,
    fresh_hbm,
    prompt_hbm,
    resident_hbm,
    absorb_hbm,
    expand_hbm,
    output_hbm,
    out,
    queries,
    spread,
    spread_rope,
    by_head,
    fresh,
    keys,
    absorb,
    expand,
    weight,
    ropes,
    asked,
    lens,
    absorbed,
    bias,
    scores,
    partial,
    stats,
    landed,
    landed_stats,
    mixed,
    landed_mixed,
    local_sem,
    block_sem,
    q_send,
    q_recv,
    n_send,
    n_recv,
    r_send,
    r_recv,
    a_send,
    a_recv,
    o_send,
    o_recv,
    t_send,
    t_recv,
    y_send,
    y_recv,
    *,
    scale,
):
    me = lax.axis_index("dev")
    held, lat, block = prompt_hbm.shape
    homes = resident_hbm.shape[0]
    prompt_rows = held * block
    home_rows = homes * block
    heads, nope, rank = absorb.shape
    requests, steps, all_heads, width = queries.shape
    own = requests * steps
    new_rows = own
    rows = DEVS * own
    span = heads * rows

    loads = [
        pltpu.make_async_copy(queries_hbm, queries, local_sem.at[0]),
        pltpu.make_async_copy(absorb_hbm, absorb, local_sem.at[1]),
        pltpu.make_async_copy(fresh_hbm, fresh, local_sem.at[2]),
        pltpu.make_async_copy(expand_hbm, expand, local_sem.at[3]),
        pltpu.make_async_copy(output_hbm, weight, local_sem.at[4]),
    ]
    blocks = [
        pltpu.make_async_copy(source.at[b], keys.at[:, pl.ds((first + b) * block, block)], block_sem.at[first + b])
        for source, count, first in ((prompt_hbm, held, 0), (resident_hbm, homes, held))
        for b in range(count)
    ]
    barrier = pltpu.get_barrier_semaphore()
    for step in range(1, DEVS):
        pl.semaphore_signal(barrier, inc=1, device_id={"dev": partner(me, step)}, device_id_type=MESH)
    for load in loads[:3]:
        load.start()

    def remote(source, target, send, recv, step):
        return pltpu.make_async_remote_copy(
            src_ref=source,
            dst_ref=target,
            send_sem=send,
            recv_sem=recv,
            device_id={"dev": partner(me, step)},
            device_id_type=MESH,
        )

    sent = []

    def launch(copy):
        copy.start()
        sent.append(copy)
        return copy

    loads[0].wait()
    for r in range(own):
        rows_now = queries[r // steps, r % steps].astype(jnp.float32)
        for ref, at in ((spread, 0), (spread_rope, nope)):
            part = rows_now[:, at : at + nope]
            if part.shape[1] < nope:
                part = jnp.concatenate([part, jnp.zeros((all_heads, nope - part.shape[1]), jnp.float32)], axis=1)
            ref[pl.ds(r, all_heads, stride=own), :] = part
    by_head[...] = spread[...].astype(jnp.bfloat16).reshape(by_head.shape)
    turned = spread_rope[:, 0 : width - nope].reshape(DEVS, heads * own, width - nope)
    middle = heads * own // 2
    ropes[0] = jnp.concatenate([turned[:, :middle], turned[:, middle:]], axis=2).astype(jnp.bfloat16)
    pl.semaphore_wait(barrier, DEVS - 1)
    asks = {}
    for step in (3, 2, 1):
        asks[step] = launch(
            remote(by_head.at[partner(me, step)], asked.at[step], q_send.at[step], q_recv.at[step], step)
        )
    for load in blocks + loads[3:]:
        load.start()
    request_row = lax.broadcasted_iota(jnp.int32, (own, 128), 0) // steps
    length_rows = jnp.zeros((own, 128), jnp.int32)
    for r in range(requests):
        length_rows = jnp.where(request_row == r, lengths[r], length_rows)
    lens[0] = length_rows
    counts = {}
    rotary = {}
    for step in (3, 2, 1):
        rotary[step] = launch(remote(ropes.at[0], ropes.at[step], r_send.at[step], r_recv.at[step], step))
    for step in (3, 2, 1):
        counts[step] = launch(remote(lens.at[0], lens.at[step], n_send.at[step], n_recv.at[step], step))

    asked[0] = by_head[me]
    loads[2].wait()
    newest = [fresh[r].astype(jnp.float32) for r in range(requests)]
    padding = jnp.zeros((block - new_rows, lat), jnp.float32)
    newest = jnp.concatenate(newest + [padding], axis=0)
    keys[:, pl.ds(prompt_rows + home_rows, block)] = jnp.transpose(newest).astype(keys.dtype)

    for step in (1, 2, 3):
        asks[step].wait_recv()
    loads[1].wait()
    asking = [asked[step].astype(jnp.float32) for step in range(DEVS)]
    shares = {}
    for head in range(heads):
        piece = jnp.concatenate([a[head * own : (head + 1) * own] for a in asking], axis=0).astype(
            jnp.bfloat16
        )
        latent = jnp.dot(piece, absorb[head], preferred_element_type=jnp.float32)
        absorbed[0, pl.ds(head * rows, rows), :] = latent.astype(jnp.bfloat16)
        part = 2 * (head + 1) // heads - 1
        if 2 * (head + 1) % heads == 0:
            at = pl.ds(part * (span // 2), span // 2)
            for step in (2, 1):
                shares[step, part] = launch(
                    remote(absorbed.at[0, at], absorbed.at[step, at], a_send.at[step, part], a_recv.at[step, part], step)
                )

    def hand_on(part):
        at = pl.ds(part * (span // 2), span // 2)
        shares[2, part].wait_recv()
        shares[3, part] = launch(
            remote(absorbed.at[2, at], absorbed.at[3, at], a_send.at[3, part], a_recv.at[3, part], 1)
        )

    for step in (1, 2, 3):
        counts[step].wait_recv()
        rotary[step].wait_recv()
    lane = lax.broadcasted_iota(jnp.int32, (rows, block), 1)
    row = lax.broadcasted_iota(jnp.int32, (rows, block), 0)
    row_length = jnp.concatenate([lens[step] for step in range(DEVS)], axis=0)
    row_device = jnp.zeros((rows, block), jnp.int32)
    for step in range(DEVS):
        row_device = jnp.where(row // own == step, partner(me, step), row_device)
    row_request = row_device * requests + (row % own) // steps
    for b in range(prompt_rows // block):
        owner = routes[0, b] * requests + routes[1, b]
        seen = (row_request == owner) & (routes[2, b] * block + lane < row_length)
        bias[:, pl.ds(b * block, block)] = jnp.where(seen, 0.0, FAR)
    for b in range(home_rows // block):
        seen = row_request == me * requests + slots[b]
        bias[:, pl.ds(prompt_rows + b * block, block)] = jnp.where(seen, 0.0, FAR)
    seen = (
        (row_request == me * requests + lane // steps)
        & (lane % steps <= row % steps)
        & (lane < new_rows)
    )
    total_rows = prompt_rows + home_rows + block
    bias[:, pl.ds(prompt_rows + home_rows, block)] = jnp.where(seen, 0.0, FAR)
    for load in blocks:
        load.wait()

    cuts = [(at, min(CHUNK, total_rows - at)) for at in range(0, total_rows, CHUNK)]
    for step in range(DEVS):
        if step == 1:
            hand_on(0)
        if step == 2:
            hand_on(1)
        if step in (1, 3):
            for part in range(2):
                shares[step, part].wait_recv()
        holder = partner(me, step)
        order = [s ^ step for s in range(DEVS)]
        turned = []
        for s in order:
            packed = ropes[s, holder].astype(jnp.float32)
            turned.append(jnp.concatenate([packed[:, : width - nope], packed[:, width - nope :]], axis=0))
        turned = jnp.concatenate(
            [a[head * own : (head + 1) * own] for head in range(heads) for a in turned], axis=0
        ).astype(jnp.bfloat16)
        shard = jnp.concatenate([absorbed[step], turned], axis=1)
        top = jnp.full((span, 1), FAR, jnp.float32)
        for at, size in cuts:
            piece = jnp.dot(shard, keys[:, pl.ds(at, size)], preferred_element_type=jnp.float32)
            mask = jnp.concatenate(
                [bias[s * own : (s + 1) * own, at : at + size] for s in order], axis=0
            )
            piece = (piece * scale).reshape(heads, rows, size) + mask[None]
            piece = piece.reshape(span, size)
            scores[:, pl.ds(at, size)] = piece
            top = jnp.maximum(top, jnp.max(piece, axis=1, keepdims=True))
        total = jnp.zeros((span, 1), jnp.float32)
        summed = jnp.zeros((span, rank), jnp.float32)
        for at, size in cuts:
            live = jnp.exp(scores[:, pl.ds(at, size)] - top)
            total = total + jnp.sum(live, axis=1, keepdims=True)
            summed = summed + lax.dot_general(
                live.astype(jnp.bfloat16),
                keys[0:rank, pl.ds(at, size)],
                (((1,), (1,)), ((), ())),
                preferred_element_type=jnp.float32,
            )
        result = (summed / total).astype(jnp.bfloat16)
        top_row = jnp.transpose(jnp.broadcast_to(top, (span, 128)))[0:8]
        total_row = jnp.transpose(jnp.broadcast_to(total, (span, 128)))[0:8]
        if step:
            partial[step] = result
            stats[step, 0:8, :] = top_row
            stats[step, 8:16, :] = total_row
            launch(remote(stats.at[step], landed_stats.at[step], t_send.at[step], t_recv.at[step], step))
            launch(remote(partial.at[step], landed.at[step], o_send.at[step], o_recv.at[step], step))
        else:
            landed[0] = result
            landed_stats[0, 0:8, :] = top_row
            landed_stats[0, 8:16, :] = total_row

    for step in (1, 3, 2):
        remote(stats.at[step], landed_stats.at[step], t_send.at[step], t_recv.at[step], step).wait_recv()
        remote(partial.at[step], landed.at[step], o_send.at[step], o_recv.at[step], step).wait_recv()
    tops = [
        jnp.transpose(jnp.broadcast_to(landed_stats[s, 0:1, :], (128, span)))[:, 0:1] for s in range(DEVS)
    ]
    totals = [
        jnp.transpose(jnp.broadcast_to(landed_stats[s, 8:9, :], (128, span)))[:, 0:1] for s in range(DEVS)
    ]
    best = functools.reduce(jnp.maximum, tops)
    parts = [t * jnp.exp(m - best) for m, t in zip(tops, totals)]
    whole = functools.reduce(jnp.add, parts)
    latent_out = functools.reduce(
        jnp.add, [landed[s].astype(jnp.float32) * (parts[s] / whole) for s in range(DEVS)]
    ).astype(jnp.bfloat16)
    loads[3].wait()
    expanded = jnp.concatenate(
        [
            jnp.dot(
                latent_out[head * rows : (head + 1) * rows],
                expand[head],
                preferred_element_type=jnp.float32,
            ).astype(jnp.bfloat16)
            for head in range(heads)
        ],
        axis=1,
    )
    loads[4].wait()
    half = out.shape[1] // 2
    pieces = y_send.shape[1]
    wide = half // pieces
    for c in range(pieces):
        low = jnp.dot(expanded, weight[:, pl.ds(c * wide, wide)], preferred_element_type=jnp.float32)
        high = jnp.dot(
            expanded, weight[:, pl.ds(half + c * wide, wide)], preferred_element_type=jnp.float32
        )
        for step in (3, 2, 1, 0):
            both = jnp.concatenate(
                [low[step * own : (step + 1) * own], high[step * own : (step + 1) * own]], axis=0
            )
            mixed[step, :, pl.ds(c * wide, wide)] = both.astype(jnp.bfloat16)
            if step:
                launch(
                    remote(
                        mixed.at[step, :, pl.ds(c * wide, wide)],
                        landed_mixed.at[step, :, pl.ds(c * wide, wide)],
                        y_send.at[step, c],
                        y_recv.at[step, c],
                        step,
                    )
                )
    for c in range(pieces):
        both = mixed[0, :, pl.ds(c * wide, wide)].astype(jnp.float32)
        for step in (1, 2, 3):
            remote(
                mixed.at[step, :, pl.ds(c * wide, wide)],
                landed_mixed.at[step, :, pl.ds(c * wide, wide)],
                y_send.at[step, c],
                y_recv.at[step, c],
                step,
            ).wait_recv()
            both = both + landed_mixed[step, :, pl.ds(c * wide, wide)].astype(jnp.float32)
        out[:, pl.ds(c * wide, wide)] = both[0:own].astype(jnp.bfloat16)
        out[:, pl.ds(half + c * wide, wide)] = both[own : 2 * own].astype(jnp.bfloat16)
    for copy in sent:
        copy.wait_send()


def still_shards(
    queries,
    new_latents,
    prompt_blocks,
    block_routes,
    prompt_lengths,
    resident_blocks,
    resident_slots,
    key_absorb,
    value_expand,
    output_weight,
):
    requests, steps, all_heads, width = queries.shape
    heads = key_absorb.shape[0]
    held, block, lat = prompt_blocks.shape
    blocks = held + resident_blocks.shape[0]
    total_rows = (blocks + 1) * block
    own = requests * steps
    rows = DEVS * own
    span = heads * rows
    rank = key_absorb.shape[2]
    model = output_weight.shape[1]
    pieces = 2
    smem = pl.BlockSpec(memory_space=pltpu.SMEM)
    vmem = pl.BlockSpec(memory_space=pltpu.VMEM)
    far = pl.BlockSpec(memory_space=pl.ANY)
    pair = pltpu.SemaphoreType.DMA((DEVS,))
    halves = pltpu.SemaphoreType.DMA((DEVS, 2))
    bf16 = jnp.bfloat16
    return pl.pallas_call(
        functools.partial(still_kernel, scale=1.0 / math.sqrt(width)),
        out_shape=jax.ShapeDtypeStruct((own, model), bf16),
        in_specs=[smem] * 3 + [far] * 7,
        out_specs=vmem,
        scratch_shapes=[
            pltpu.VMEM(queries.shape, bf16),
            pltpu.VMEM((own * all_heads, 128), jnp.float32),
            pltpu.VMEM((own * all_heads, 128), jnp.float32),
            pltpu.VMEM((DEVS, heads * own, key_absorb.shape[1]), bf16),
            pltpu.VMEM(new_latents.shape, bf16),
            pltpu.VMEM((lat, total_rows), bf16),
            pltpu.VMEM(key_absorb.shape, bf16),
            pltpu.VMEM(value_expand.shape, bf16),
            pltpu.VMEM(output_weight.shape, bf16),
            pltpu.VMEM((DEVS, DEVS, heads * own // 2, 2 * (width - key_absorb.shape[1])), bf16),
            pltpu.VMEM((DEVS, heads * own, key_absorb.shape[1]), bf16),
            pltpu.VMEM((DEVS, own, 128), jnp.int32),
            pltpu.VMEM((DEVS, span, rank), bf16),
            pltpu.VMEM((rows, total_rows), jnp.float32),
            pltpu.VMEM((span, total_rows), jnp.float32),
            pltpu.VMEM((DEVS, span, rank), bf16),
            pltpu.VMEM((DEVS, 16, span), jnp.float32),
            pltpu.VMEM((DEVS, span, rank), bf16),
            pltpu.VMEM((DEVS, 16, span), jnp.float32),
            pltpu.VMEM((DEVS, 2 * own, model // 2), bf16),
            pltpu.VMEM((DEVS, 2 * own, model // 2), bf16),
            pltpu.SemaphoreType.DMA((5,)),
            pltpu.SemaphoreType.DMA((blocks,)),
            pair,
            pair,
            pair,
            pair,
            pair,
            pair,
            halves,
            halves,
            pair,
            pair,
            pair,
            pair,
            pltpu.SemaphoreType.DMA((DEVS, pieces)),
            pltpu.SemaphoreType.DMA((DEVS, pieces)),
        ],
        compiler_params=pltpu.CompilerParams(
            collective_id=0, has_side_effects=True, vmem_limit_bytes=63 * 1024 * 1024
        ),
        name="still_attention",
    )(
        block_routes.T,
        resident_slots,
        prompt_lengths,
        queries,
        new_latents,
        prompt_blocks.transpose(0, 2, 1),
        resident_blocks.transpose(0, 2, 1),
        key_absorb,
        value_expand,
        output_weight,
    )


def solution(mesh):
    body = still_shards if mesh.shape["dev"] == DEVS else routed_shards
    in_specs = (
        P(("groups", "dev", "pd"), None, None, None),
        P(("groups", "dev", "pd"), None, None),
        P(("groups", "dev", "pd"), None, None),
        P(("groups", "dev", "pd"), None),
        P(("groups", "dev", "pd")),
        P(("groups", "dev", "pd"), None, None),
        P(("groups", "dev", "pd")),
        P("dev", None, None),
        P("dev", None, None),
        P("dev", None),
    )
    out_specs = P(("groups", "dev", "pd"), None)
    return jax.shard_map(body, mesh=mesh, in_specs=in_specs, out_specs=out_specs, check_vma=False)
```
